128 devices in a mesh: row: 16 (over z, y), col: 8 (over x, core).
Axes of the slice: x: 4, y: 4, z: 4, core: 2. Of those that a mesh axis runs over, the one named last changes fastest.
Arguments:
- sub_field: float32 [262144, 128], P(('row', 'col')), may hold values from -2.4 to 2.4
- reluctivity: float32 [2, 262144, 128], P(None, ('row', 'col')), may hold values from 0.3 to 3
- stride: int32 [128], P(('row', 'col')), may hold values from 2 to 511
- counts: int32 [128, 16], P(('row', 'col')), may hold values from 1 to 32, as said below
- source_cell: int32 [128, 16, 32], P(('row', 'col')), may hold values from 0 to 2047
- target_row: int32 [16, 8, 16, 32], P('row', 'col'), may hold values from 0 to 2047
- lower_tiles: float32 [28, 4096, 4096], P(None, 'row', 'col'), may hold values from -0.03125 to 0.03125
- diag_inverse: float32 [8, 4096, 4096], P(None, 'col', 'row'), may hold values from -1 to 2, as said below
Outputs:
- solution: float32 [8, 8, 512, 128], P(None, 'col', 'row')
The draws below stay inside these ranges and needn't reach their ends.
Inputs may be any that keep to these rules, and one draw needn't show every extreme that they name: `counts`: every subdomain sends at least one contribution to every grid row; in every draw one grid row receives 32 contributions from every subdomain. `diag_inverse`: block i is the given inverse of the window's diagonal block i.
All inputs are finite; a program needn't handle non-finite values.
Results may differ from the reference program's by a relative error of at most 0.0003.
Values sent between devices are 32-bit elements; how exact they have to be, the bound alone decides.
No kernel may reach another device: no remote copies, remote signals or barrier semaphores. Data moves between devices by JAX's collectives and lax.ppermute only.
A program may use at most 128 MiB of HBM per device.

```python
import math
import jax
import jax.numpy as jnp
from jax import lax

R = 128
TB = 256
WIN = 8
SC = 2048
CAP = 32
NB = 4096
CB = 512
PAIRS = 28
NSUB = 128
N_ROW = 16
N_COL = 8


def draw_counts(key, part):
    first_key, second_key = jax.random.split(key)
    hottest = jax.random.randint(first_key, (), 0, N_ROW)
    base_counts = jax.random.randint(second_key, (NSUB, N_ROW), 1, CAP + 1)
    columns = jnp.arange(N_ROW, dtype=jnp.int32)[None, :]
    return jnp.where(columns == hottest, CAP, base_counts).astype(jnp.int32)


def draw_diag_inverse(key, part):
    first_key, second_key = jax.random.split(key)
    rows = jnp.arange(NB, dtype=jnp.int32)[:, None]
    columns = jnp.arange(NB, dtype=jnp.int32)[None, :]
    identity = (rows == columns).astype(jnp.float32)
    spread = jax.random.normal(first_key, (WIN, NB, NB), jnp.float32) * (0.45 / NB ** 0.5)
    diagonal = jax.random.uniform(second_key, (WIN, NB), jnp.float32, 0.8, 1.2)
    return (spread + identity[None, :, :] * diagonal[:, :, None]).astype(jnp.float32)


def plant(entries, stream_key, smallest, top_value):
    longest = entries.shape.index(max(entries.shape))
    spots = []
    for shift in (0, 1):
        where = [jax.random.randint(jax.random.fold_in(stream_key, axis), (), 0, length) for axis, length in enumerate(entries.shape)]
        where[longest] = (where[longest] + shift) % entries.shape[longest]
        spots.append(tuple(where))
    return entries.at[spots[0]].set(smallest).at[spots[1]].set(top_value)


def shard_levels(key, shape, cuts, low, largest):
    def one(axis_at, shards_of):
        steps = jax.random.uniform(jax.random.fold_in(jax.random.fold_in(key, 6), axis_at), (shards_of,), jnp.float32, low / len(cuts), largest / len(cuts))
        return jnp.repeat(jnp.exp(steps), shape[axis_at] // shards_of).reshape((-1,) + (1,) * (len(shape) - axis_at - 1))

    level = one(*cuts[0])
    for cut in cuts[1:]:
        level = level * one(*cut)
    return level


def scatter_about(key, extent, scale, bound, shards=(), held_as=jnp.bfloat16):
    level = shard_levels(key, extent, shards, -0.22, 0.18) if shards else 1.0
    entries = jax.random.normal(key, extent, jnp.float32) * scale * level
    return jnp.minimum(jnp.maximum(entries, -bound), bound).astype(held_as)


def setup_inputs(seed: int = 0) -> dict:
    splits = jax.random.split(jax.random.key(seed), 9)
    return {
        "sub_field": scatter_about(splits[0], (NSUB * SC, R), 0.4, 2.4, ((0, 128),), jnp.float32),
        "reluctivity": jnp.clip(jnp.exp(math.log(3.0) - 2.3025851 * jax.random.uniform(splits[1], (2, NSUB * SC, R), jnp.float32) ** shard_levels(splits[1], (2, NSUB * SC, R), ((1, 128),), -0.2, 0.2)), 0.3, 3.0),
        "stride": plant(jax.random.randint(splits[2], (NSUB,), 2, SC // 4), jax.random.fold_in(splits[2], 1), 2, (SC // 4) - 1).astype(jnp.int32),
        "counts": draw_counts(jax.random.fold_in(splits[8], 71), 0),
        "source_cell": plant(jax.random.randint(splits[4], (NSUB, N_ROW, CAP), 0, SC), jax.random.fold_in(splits[4], 1), 0, SC - 1).astype(jnp.int32),
        "target_row": plant(jax.random.randint(splits[5], (N_ROW, N_COL, N_ROW, CAP), 0, WIN * TB), jax.random.fold_in(splits[5], 1), 0, (WIN * TB) - 1).astype(jnp.int32),
        "lower_tiles": scatter_about(splits[6], (PAIRS, NB, NB), (NB * WIN) ** -0.5, 0.03125, ((1, 16), (2, 8)), jnp.float32),
        "diag_inverse": draw_diag_inverse(jax.random.fold_in(splits[8], 71), 0),
    }


def sweep_subdomain(field, radial_nu, tangent_nu, stride_value):
    cell_index = jnp.arange(field.shape[0], dtype=jnp.int32)[:, None]
    radial_prev = jnp.where(cell_index >= stride_value, jnp.roll(field, stride_value, axis=0), 0.0)
    tangent_prev = jnp.where(cell_index >= 1, jnp.roll(field, 1, axis=0), 0.0)
    return radial_nu * (field - radial_prev) + tangent_nu * (field - tangent_prev)


def exact_dot(left, right):
    return jnp.dot(left, right, precision=lax.Precision.HIGHEST, preferred_element_type=jnp.float32)


def reference(sub_field, reluctivity, stride, counts, source_cell, target_row, lower_tiles, diag_inverse):
    subdomains = N_ROW * N_COL
    fields = sub_field.reshape(subdomains, SC, R)
    coefficients = reluctivity.reshape(2, subdomains, SC, R)
    swept = jax.vmap(sweep_subdomain)(fields, coefficients[0], coefficients[1], stride)
    owners = jnp.arange(subdomains, dtype=jnp.int32)[:, None, None]
    picked = swept[owners, source_cell]
    live = jnp.arange(CAP, dtype=jnp.int32)[None, None, :] < counts[:, :, None]
    picked = jnp.where(live[:, :, :, None], picked, 0.0)
    targets = jnp.transpose(target_row, (2, 1, 0, 3)).reshape(subdomains, N_ROW, CAP)
    grid_index = jnp.arange(N_ROW, dtype=jnp.int32)[None, :, None]
    global_row = (targets // TB) * NB + grid_index * TB + targets % TB
    rhs = jnp.zeros((WIN * NB, R), jnp.float32).at[global_row.reshape(-1)].add(picked.reshape(-1, R))
    rhs = rhs.reshape(WIN, NB, R)
    solved = []
    for row_block in range(WIN):
        residual = rhs[row_block]
        for earlier in range(row_block):
            residual = residual - exact_dot(lower_tiles[row_block * (row_block - 1) // 2 + earlier], solved[earlier])
        solved.append(exact_dot(diag_inverse[row_block], residual))
    return jnp.stack(solved).reshape(WIN, N_COL, CB, R)
```

```python
import jax
import jax.numpy as jnp
from jax import lax
from jax.sharding import PartitionSpec as P


def product(left, right, precision=lax.Precision.HIGH):
    return jnp.dot(left, right, precision=precision, preferred_element_type=jnp.float32)


def sweep_subdomain(field, radial_nu, tangent_nu, stride_value):
    cell_index = jnp.arange(field.shape[0], dtype=jnp.int32)[:, None]
    radial_prev = jnp.where(cell_index >= stride_value, jnp.roll(field, stride_value, axis=0), 0.0)
    tangent_prev = jnp.where(cell_index >= 1, jnp.roll(field, 1, axis=0), 0.0)
    return radial_nu * (field - radial_prev) + tangent_nu * (field - tangent_prev)


def pair_index(later_block, earlier_block):
    return later_block * (later_block - 1) // 2 + earlier_block


def other_core(value):
    peers = lax.axis_size("col")
    return lax.ppermute(value, "col", [(i, i ^ 1) for i in range(peers)])


def total_along_x(value):
    peers = lax.axis_size("col")
    arrived = [
        lax.ppermute(value, "col", [(i, (i + hop) % peers) for i in range(peers)])
        for hop in range(2, peers, 2)
    ]
    for part in arrived:
        value = value + part
    return value


def column_total(partial_rows):
    core = lax.axis_index("col") % 2
    half = partial_rows.shape[0] // 2
    low, high = partial_rows[:half], partial_rows[half:]
    mine = jnp.where(core == 0, low, high)
    theirs = jnp.where(core == 0, high, low)
    mine = total_along_x(mine + other_core(theirs))
    theirs = other_core(mine)
    return jnp.concatenate(
        [jnp.where(core == 0, mine, theirs), jnp.where(core == 0, theirs, mine)], axis=0
    )


def row_share(partial_share):
    peers = lax.axis_size("row")
    tiles = partial_share.reshape(peers, -1, partial_share.shape[1])
    return jnp.sum(lax.all_to_all(tiles, "row", 0, 0, tiled=True), axis=0)


def row_gather(piece):
    peers = lax.axis_size("row")
    copies = jnp.broadcast_to(piece, (peers, *piece.shape))
    return lax.all_to_all(copies, "row", 0, 0, tiled=True).reshape(-1, piece.shape[1])


def per_device(
    sub_field, reluctivity, stride, counts, source_cell, target_row, lower_tiles, diag_inverse
):
    blocks = diag_inverse.shape[0]
    tile_rows = lower_tiles.shape[1]
    rotor = sub_field.shape[1]
    swept = sweep_subdomain(sub_field, reluctivity[0], reluctivity[1], stride[0])
    picked = swept[source_cell[0]]
    slots = source_cell.shape[2]
    live = jnp.arange(slots, dtype=jnp.int32)[None, :] < counts[0][:, None]
    picked = jnp.where(live[:, :, None], picked, 0.0)
    received = lax.all_to_all(picked, "row", split_axis=0, concat_axis=0, tiled=True)
    received = received.reshape(-1, rotor)
    targets = target_row[0, 0].reshape(1, -1)

    def interface(block):
        rows = block * tile_rows + jnp.arange(tile_rows, dtype=jnp.int32)[:, None]
        return product(
            (rows == targets).astype(jnp.float32), received, lax.Precision.HIGHEST
        )

    shares = []
    pieces = []
    pending = interface(0)
    for block in range(blocks):
        residual = column_total(pending)
        piece = row_share(product(diag_inverse[block], residual))
        pieces.append(piece)
        if block + 1 < blocks:
            started = interface(block + 1)
            for earlier in range(block):
                started = started - product(
                    lower_tiles[pair_index(block + 1, earlier)], shares[earlier]
                )
            shares.append(row_gather(piece))
            pending = started - product(lower_tiles[pair_index(block + 1, block)], shares[block])
    return jnp.stack(pieces)[:, None]


def solution(mesh):
    placed = (
        P(("row", "col"), None),
        P(None, ("row", "col"), None),
        P(("row", "col")),
        P(("row", "col"), None),
        P(("row", "col"), None, None),
        P("row", "col", None, None),
        P(None, "row", "col"),
        P(None, "col", "row"),
    )
    return jax.shard_map(
        per_device,
        mesh=mesh,
        in_specs=placed,
        out_specs=P(None, "col", "row", None),
        check_vma=False,
    )
```

```python
import functools

import jax
import jax.numpy as jnp
from jax import lax
from jax.experimental import pallas as pl
from jax.experimental.pallas import tpu as pltpu
from jax.sharding import PartitionSpec as P

F32 = jnp.float32
BF16 = jnp.bfloat16
VMEM_LIMIT = 32 * 1024 * 1024
VMEM = pl.BlockSpec(memory_space=pltpu.VMEM)
SMEM = pl.BlockSpec(memory_space=pltpu.SMEM)
ANY = pl.BlockSpec(memory_space=pl.ANY)


def kernel_params():
    return pltpu.CompilerParams(vmem_limit_bytes=VMEM_LIMIT)


def dot(left, right):
    return jnp.dot(left, right, preferred_element_type=F32)


def split(value):
    high = value.astype(BF16)
    return high, (value - high.astype(F32)).astype(BF16)


def split_product(left_high, left_low, right):
    width = right.shape[1]
    high, low = split(right)
    both = dot(left_high, jnp.concatenate([high, low], axis=1))
    return both[:, :width] + both[:, width:] + dot(left_low, high)


def pick_kernel(stride_ref, counts_ref, source_ref, field_hbm, nu_hbm, out_ref, field, nu, sems):
    cells = nu.shape[1]
    pad = field.shape[0] - cells
    loads = [
        pltpu.make_async_copy(field_hbm, field.at[pl.ds(pad, cells)], sems.at[0]),
        pltpu.make_async_copy(nu_hbm, nu, sems.at[1]),
    ]
    for load in loads:
        load.start()
    field[0:pad, :] = jnp.zeros((pad, field.shape[1]), F32)
    for load in loads:
        load.wait()
    stride = stride_ref[0]
    slots = source_ref.shape[2]

    @pl.loop(0, source_ref.shape[1])
    def _(grid_row):
        live = counts_ref[0, grid_row]
        for slot in range(slots):
            cell = source_ref[0, grid_row, slot]
            here = field[pl.ds(pad + cell, 1), :]
            radial = here - field[pl.ds(pad + cell - stride, 1), :]
            tangent = here - field[pl.ds(pad - 1 + cell, 1), :]
            swept = nu[0, pl.ds(cell, 1), :] * radial + nu[1, pl.ds(cell, 1), :] * tangent
            out_ref[grid_row, pl.ds(slot, 1), :] = jnp.where(slot < live, swept, 0.0)


def pick(sub_field, reluctivity, stride, counts, source_cell):
    cells, rotor = sub_field.shape
    _, grid_rows, slots = source_cell.shape
    pad = 512
    return pl.pallas_call(
        pick_kernel,
        out_shape=jax.ShapeDtypeStruct((grid_rows, slots, rotor), F32),
        in_specs=[SMEM, SMEM, SMEM, ANY, ANY],
        out_specs=VMEM,
        scratch_shapes=[
            pltpu.VMEM((pad + cells, rotor), F32),
            pltpu.VMEM((2, cells, rotor), F32),
            pltpu.SemaphoreType.DMA((2,)),
        ],
        compiler_params=kernel_params(),
        name="pick",
    )(stride, counts, source_cell, sub_field, reluctivity)


def interface_rows(block, rows, targets_ref, received_ref):
    received = received_ref[...]
    high, low = split(received)
    rest = (received - high.astype(F32) - low.astype(F32)).astype(BF16)
    row = block * rows + lax.broadcasted_iota(jnp.int32, (rows, received.shape[0]), 0)
    chosen = jnp.where(row == targets_ref[...], 1.0, 0.0).astype(BF16)
    both = dot(chosen, jnp.concatenate([high, low], axis=1))
    width = received.shape[1]
    return both[:, :width] + both[:, width:] + dot(chosen, rest)


def halves_out(core_ref, value, mine_ref, theirs_ref, whole):
    whole[...] = value
    half = mine_ref.shape[0]
    core = core_ref[0]
    mine_ref[...] = whole[pl.ds(pl.multiple_of(core * half, half), half), :]
    theirs_ref[...] = whole[pl.ds(pl.multiple_of((1 - core) * half, half), half), :]


def half_shapes(rows, rotor):
    return [jax.ShapeDtypeStruct((rows // 2, rotor), F32)] * 2


def first_kernel(core_ref, targets_ref, received_ref, mine_ref, theirs_ref, whole):
    rows = whole.shape[0]
    value = interface_rows(0, rows, targets_ref, received_ref)
    halves_out(core_ref, value, mine_ref, theirs_ref, whole)


def first_residual(core, targets, received, rows):
    rotor = received.shape[1]
    return pl.pallas_call(
        first_kernel,
        out_shape=half_shapes(rows, rotor),
        in_specs=[SMEM, VMEM, VMEM],
        out_specs=[VMEM, VMEM],
        scratch_shapes=[pltpu.VMEM((rows, rotor), F32)],
        compiler_params=kernel_params(),
        name="first",
    )(core, targets, received)


def fold_kernel(block, first, *refs):
    earlier = block - 1
    targets_ref, received_ref, lower_hbm, diag_hbm = refs[:4]
    shares = refs[4 : 4 + earlier]
    outs = refs[4 + earlier : -3]
    tiles, diags, sems = refs[-3:]
    base = block * (block - 1) // 2
    loads = [
        pltpu.make_async_copy(lower_hbm.at[base + j], tiles.at[j], sems.at[j])
        for j in range(block)
    ]
    loads += [
        pltpu.make_async_copy(diag_hbm.at[first + j], diags.at[j], sems.at[block + j])
        for j in range(block - first + 1)
    ]
    for load in loads:
        load.start()
    started_ref, lower_high, lower_low = outs[:3]
    total = interface_rows(block, started_ref.shape[0], targets_ref, received_ref)
    for j in range(earlier):
        loads[j].wait()
        high, low = split(tiles[j])
        total = total - split_product(high, low, shares[j][...])
    started_ref[...] = total
    loads[earlier].wait()
    lower_high[...], lower_low[...] = split(tiles[earlier])
    for j in range(block - first + 1):
        loads[block + j].wait()
        outs[3 + 2 * j][...], outs[4 + 2 * j][...] = split(diags[j])


def fold(block, first, targets, received, lower_tiles, diag_inverse, shares):
    _, rows, columns = lower_tiles.shape
    _, out_rows, depth = diag_inverse.shape
    rotor = received.shape[1]
    n_diag = block - first + 1
    shapes = [jax.ShapeDtypeStruct((rows, rotor), F32)]
    shapes += [jax.ShapeDtypeStruct((rows, columns), BF16)] * 2
    shapes += [jax.ShapeDtypeStruct((out_rows, depth), BF16)] * (2 * n_diag)
    return pl.pallas_call(
        functools.partial(fold_kernel, block, first),
        out_shape=shapes,
        in_specs=[VMEM, VMEM, ANY, ANY] + [VMEM] * len(shares),
        out_specs=[VMEM] * len(shapes),
        scratch_shapes=[
            pltpu.VMEM((block, rows, columns), F32),
            pltpu.VMEM((n_diag, out_rows, depth), F32),
            pltpu.SemaphoreType.DMA((block + n_diag,)),
        ],
        compiler_params=kernel_params(),
        cost_estimate=pl.CostEstimate(
            flops=6 * block * rows * columns * rotor,
            bytes_accessed=4 * (block + n_diag) * rows * columns,
            transcendentals=0,
        ),
        name="fold",
    )(targets, received, lower_tiles, diag_inverse, *shares)


def lower_kernel(core_ref, share_ref, high_ref, low_ref, started_ref, mine_ref, theirs_ref, whole):
    value = started_ref[...] - split_product(high_ref[...], low_ref[...], share_ref[...])
    halves_out(core_ref, value, mine_ref, theirs_ref, whole)


def lower_product(core, share, high, low, started):
    rows, rotor = started.shape
    return pl.pallas_call(
        lower_kernel,
        out_shape=half_shapes(rows, rotor),
        in_specs=[SMEM] + [VMEM] * 4,
        out_specs=[VMEM, VMEM],
        scratch_shapes=[pltpu.VMEM((rows, rotor), F32)],
        compiler_params=kernel_params(),
        name="lower",
    )(core, share, high, low, started)


def diag_kernel(core_ref, mine_ref, theirs_ref, high_ref, low_ref, out_ref, whole):
    half = mine_ref.shape[0]
    core = core_ref[0]
    whole[pl.ds(pl.multiple_of(core * half, half), half), :] = mine_ref[...]
    whole[pl.ds(pl.multiple_of((1 - core) * half, half), half), :] = theirs_ref[...]
    out_ref[...] = split_product(high_ref[...], low_ref[...], whole[...])


def diag_product(core, mine, theirs, high, low):
    half, rotor = mine.shape
    return pl.pallas_call(
        diag_kernel,
        out_shape=jax.ShapeDtypeStruct((high.shape[0], rotor), F32),
        in_specs=[SMEM] + [VMEM] * 4,
        out_specs=VMEM,
        scratch_shapes=[pltpu.VMEM((2 * half, rotor), F32)],
        compiler_params=kernel_params(),
        name="diag",
    )(core, mine, theirs, high, low)


def piece_kernel(parts_ref, piece_ref, copies_ref):
    piece = jnp.sum(parts_ref[...], axis=0)
    piece_ref[...] = piece
    for peer in range(copies_ref.shape[0]):
        copies_ref[peer] = piece


def piece_and_copies(parts):
    return pl.pallas_call(
        piece_kernel,
        out_shape=[
            jax.ShapeDtypeStruct(parts.shape[1:], F32),
            jax.ShapeDtypeStruct(parts.shape, F32),
        ],
        in_specs=[VMEM],
        out_specs=[VMEM, VMEM],
        compiler_params=kernel_params(),
        name="piece",
    )(parts)


def other_core(value):
    peers = lax.axis_size("col")
    return lax.ppermute(value, "col", [(i, i ^ 1) for i in range(peers)])


def total_along_x(value):
    peers = lax.axis_size("col")
    arrived = [
        lax.ppermute(value, "col", [(i, (i + hop) % peers) for i in range(peers)])
        for hop in range(2, peers, 2)
    ]
    for part in arrived:
        value = value + part
    return value


def per_row(value):
    return lax.all_to_all(value, "row", 0, 0, tiled=True)


def per_device(
    sub_field, reluctivity, stride, counts, source_cell, target_row, lower_tiles, diag_inverse
):
    blocks = diag_inverse.shape[0]
    tile_rows = lower_tiles.shape[1]
    rotor = sub_field.shape[1]
    peers = lax.axis_size("row")
    core = (lax.axis_index("col") % 2).astype(jnp.int32).reshape(1)
    received = per_row(pick(sub_field, reluctivity, stride, counts, source_cell))
    received = received.reshape(-1, rotor)
    targets = target_row.reshape(1, -1)

    shares = []
    pieces = []
    mine, theirs = first_residual(core, targets, received, tile_rows)
    for block in range(blocks):
        mine = total_along_x(mine + other_core(theirs))
        if block + 1 < blocks:
            started, lower_high, lower_low, *diags = fold(
                block + 1,
                block + 1 if block else 0,
                targets,
                received,
                lower_tiles,
                diag_inverse,
                shares,
            )
            if block == 0:
                diag_high, diag_low, *diags = diags
        partial = diag_product(core, mine, other_core(mine), diag_high, diag_low)
        parts = per_row(partial.reshape(peers, -1, rotor))
        piece, copies = piece_and_copies(parts)
        pieces.append(piece)
        if block + 1 < blocks:
            share = per_row(copies).reshape(-1, rotor)
            shares.append(share)
            mine, theirs = lower_product(core, share, lower_high, lower_low, started)
            diag_high, diag_low = diags
    return jnp.stack(pieces)[:, None]


def solution(mesh):
    placed = (
        P(("row", "col"), None),
        P(None, ("row", "col"), None),
        P(("row", "col")),
        P(("row", "col"), None),
        P(("row", "col"), None, None),
        P("row", "col", None, None),
        P(None, "row", "col"),
        P(None, "col", "row"),
    )
    return jax.shard_map(
        per_device,
        mesh=mesh,
        in_specs=placed,
        out_specs=P(None, "col", "row", None),
        check_vma=False,
    )
```

```python
import functools

import jax
import jax.numpy as jnp
from jax import lax
from jax.experimental import pallas as pl
from jax.experimental.pallas import tpu as pltpu
from jax.sharding import PartitionSpec as P

F32 = jnp.float32
BF16 = jnp.bfloat16
VMEM_LIMIT = 32 * 1024 * 1024
WIDE_LIMIT = 50 * 1024 * 1024
PICK_LIMIT = 54 * 1024 * 1024
VMEM = pl.BlockSpec(memory_space=pltpu.VMEM)
SMEM = pl.BlockSpec(memory_space=pltpu.SMEM)
HBM = pl.BlockSpec(memory_space=pltpu.HBM)


def kernel_params(limit=VMEM_LIMIT):
    return pltpu.CompilerParams(vmem_limit_bytes=limit)


def dot(left, right):
    return jnp.dot(left, right, preferred_element_type=F32)


def split(value):
    high = value.astype(BF16)
    return high, (value - high.astype(F32)).astype(BF16)


def split_product(left_high, left_low, right):
    width = right.shape[1]
    high, low = split(right)
    both = dot(left_high, jnp.concatenate([high, low], axis=1))
    return both[:, :width] + both[:, width:] + dot(left_low, high)


def pick_kernel(
    stride_hbm, counts_hbm, source_hbm, target_ref, field_hbm, nu_hbm,
    out_ref, targets_ref, stride_ref, counts_ref, source_ref, field, nu, sems,
):
    cells = nu.shape[1]
    pad = field.shape[0] - cells
    loads = [
        pltpu.make_async_copy(stride_hbm, stride_ref, sems.at[2]),
        pltpu.make_async_copy(counts_hbm, counts_ref, sems.at[3]),
        pltpu.make_async_copy(source_hbm, source_ref, sems.at[4]),
        pltpu.make_async_copy(field_hbm, field.at[pl.ds(pad, cells)], sems.at[0]),
        pltpu.make_async_copy(nu_hbm, nu, sems.at[1]),
    ]
    for load in loads:
        load.start()
    field[0:pad, :] = jnp.zeros((pad, field.shape[1]), F32)
    width = target_ref.shape[1]
    for sender in range(target_ref.shape[0]):
        targets_ref[0:1, sender * width : (sender + 1) * width] = target_ref[sender : sender + 1, :]
    for load in loads:
        load.wait()
    stride = stride_ref[0]
    slots = source_ref.shape[2]

    @pl.loop(0, source_ref.shape[1])
    def _(grid_row):
        live = counts_ref[0, grid_row]
        for slot in range(slots):
            cell = source_ref[0, grid_row, slot]
            here = field[pl.ds(pad + cell, 1), :]
            radial = here - field[pl.ds(pad + cell - stride, 1), :]
            tangent = here - field[pl.ds(pad - 1 + cell, 1), :]
            swept = nu[0, pl.ds(cell, 1), :] * radial + nu[1, pl.ds(cell, 1), :] * tangent
            out_ref[grid_row, pl.ds(slot, 1), :] = jnp.where(slot < live, swept, 0.0)


def pick(sub_field, reluctivity, stride, counts, source_cell, target_row):
    cells, rotor = sub_field.shape
    _, grid_rows, slots = source_cell.shape
    pad = 512
    return pl.pallas_call(
        pick_kernel,
        out_shape=[
            jax.ShapeDtypeStruct((grid_rows, slots, rotor), F32),
            jax.ShapeDtypeStruct((1, target_row.size), jnp.int32),
        ],
        in_specs=[HBM, HBM, HBM, VMEM, HBM, HBM],
        out_specs=[VMEM, VMEM],
        scratch_shapes=[
            pltpu.SMEM(stride.shape, jnp.int32),
            pltpu.SMEM(counts.shape, jnp.int32),
            pltpu.SMEM(source_cell.shape, jnp.int32),
            pltpu.VMEM((pad + cells, rotor), F32),
            pltpu.VMEM((2, cells, rotor), F32),
            pltpu.SemaphoreType.DMA((5,)),
        ],
        compiler_params=kernel_params(PICK_LIMIT),
        name="pick",
    )(stride, counts, source_cell, target_row, sub_field, reluctivity)


def interface_rows(block, rows, targets_ref, received_ref):
    received = received_ref[...]
    high, low = split(received)
    rest = (received - high.astype(F32) - low.astype(F32)).astype(BF16)
    row = block * rows + lax.broadcasted_iota(jnp.int32, (rows, received.shape[0]), 0)
    chosen = jnp.where(row == targets_ref[...], 1.0, 0.0).astype(BF16)
    both = dot(chosen, jnp.concatenate([high, low], axis=1))
    width = received.shape[1]
    return both[:, :width] + both[:, width:] + dot(chosen, rest)


def halves_out(core_ref, value, mine_ref, theirs_ref, whole):
    whole[...] = value
    half = mine_ref.shape[0]
    core = core_ref[0]
    mine_ref[...] = whole[pl.ds(pl.multiple_of(core * half, half), half), :]
    theirs_ref[...] = whole[pl.ds(pl.multiple_of((1 - core) * half, half), half), :]


def half_shapes(rows, rotor):
    return [jax.ShapeDtypeStruct((rows // 2, rotor), F32)] * 2


def first_kernel(core_ref, targets_ref, received_ref, mine_ref, theirs_ref, whole):
    rows = whole.shape[0]
    value = interface_rows(0, rows, targets_ref, received_ref)
    halves_out(core_ref, value, mine_ref, theirs_ref, whole)


def first_residual(core, targets, received, rows):
    rotor = received.shape[1]
    return pl.pallas_call(
        first_kernel,
        out_shape=half_shapes(rows, rotor),
        in_specs=[SMEM, VMEM, VMEM],
        out_specs=[VMEM, VMEM],
        scratch_shapes=[pltpu.VMEM((rows, rotor), F32)],
        compiler_params=kernel_params(),
        name="first",
    )(core, targets, received)


def fold_kernel(block, first, last, *refs):
    earlier = block - 1
    targets_ref, received_ref, lower_hbm, diag_hbm = refs[:4]
    shares = refs[4 : 4 + earlier]
    outs = refs[4 + earlier : -3]
    tiles, diags, sems = refs[-3:]
    base = block * (block - 1) // 2
    loads = [
        pltpu.make_async_copy(lower_hbm.at[base + j], tiles.at[j], sems.at[j])
        for j in range(block)
    ]
    loads += [
        pltpu.make_async_copy(diag_hbm.at[first + j], diags.at[j], sems.at[block + j])
        for j in range(last - first + 1)
    ]
    for load in loads:
        load.start()
    started_ref, lower_high, lower_low = outs[:3]
    total = interface_rows(block, started_ref.shape[0], targets_ref, received_ref)
    for j in range(earlier):
        loads[j].wait()
        high, low = split(tiles[j])
        total = total - split_product(high, low, shares[j][...])
    started_ref[...] = total
    loads[earlier].wait()
    lower_high[...], lower_low[...] = split(tiles[earlier])
    for j in range(last - first + 1):
        loads[block + j].wait()
        outs[3 + 2 * j][...], outs[4 + 2 * j][...] = split(diags[j])


def fold(block, first, last, targets, received, lower_tiles, diag_inverse, shares):
    _, rows, columns = lower_tiles.shape
    _, out_rows, depth = diag_inverse.shape
    rotor = received.shape[1]
    n_diag = last - first + 1
    shapes = [jax.ShapeDtypeStruct((rows, rotor), F32)]
    shapes += [jax.ShapeDtypeStruct((rows, columns), BF16)] * 2
    shapes += [jax.ShapeDtypeStruct((out_rows, depth), BF16)] * (2 * n_diag)
    return pl.pallas_call(
        functools.partial(fold_kernel, block, first, last),
        out_shape=shapes,
        in_specs=[VMEM, VMEM, HBM, HBM] + [VMEM] * len(shares),
        out_specs=[VMEM] * len(shapes),
        scratch_shapes=[
            pltpu.VMEM((block, rows, columns), F32),
            pltpu.VMEM((n_diag, out_rows, depth), F32),
            pltpu.SemaphoreType.DMA((block + n_diag,)),
        ],
        compiler_params=kernel_params(WIDE_LIMIT),
        cost_estimate=pl.CostEstimate(
            flops=6 * block * rows * columns * rotor,
            bytes_accessed=4 * (block + n_diag) * rows * columns,
            transcendentals=0,
        ),
        name="fold",
    )(targets, received, lower_tiles, diag_inverse, *shares)


def lower_kernel(core_ref, share_ref, high_ref, low_ref, started_ref, mine_ref, theirs_ref, whole):
    value = started_ref[...] - split_product(high_ref[...], low_ref[...], share_ref[...])
    halves_out(core_ref, value, mine_ref, theirs_ref, whole)


def lower_product(core, share, high, low, started):
    rows, rotor = started.shape
    return pl.pallas_call(
        lower_kernel,
        out_shape=half_shapes(rows, rotor),
        in_specs=[SMEM] + [VMEM] * 4,
        out_specs=[VMEM, VMEM],
        scratch_shapes=[pltpu.VMEM((rows, rotor), F32)],
        compiler_params=kernel_params(),
        name="lower",
    )(core, share, high, low, started)


def diag_kernel(core_ref, mine_ref, theirs_ref, high_ref, low_ref, out_ref, whole):
    half = mine_ref.shape[0]
    core = core_ref[0]
    whole[pl.ds(pl.multiple_of(core * half, half), half), :] = mine_ref[...]
    whole[pl.ds(pl.multiple_of((1 - core) * half, half), half), :] = theirs_ref[...]
    out_ref[...] = split_product(high_ref[...], low_ref[...], whole[...])


def diag_product(core, mine, theirs, high, low):
    half, rotor = mine.shape
    return pl.pallas_call(
        diag_kernel,
        out_shape=jax.ShapeDtypeStruct((high.shape[0], rotor), F32),
        in_specs=[SMEM] + [VMEM] * 4,
        out_specs=VMEM,
        scratch_shapes=[pltpu.VMEM((2 * half, rotor), F32)],
        compiler_params=kernel_params(),
        name="diag",
    )(core, mine, theirs, high, low)


def piece_kernel(parts_ref, piece_ref, copies_ref):
    piece = jnp.sum(parts_ref[...], axis=0)
    piece_ref[...] = piece
    for peer in range(copies_ref.shape[0]):
        copies_ref[peer] = piece


def piece_and_copies(parts):
    return pl.pallas_call(
        piece_kernel,
        out_shape=[
            jax.ShapeDtypeStruct(parts.shape[1:], F32),
            jax.ShapeDtypeStruct(parts.shape, F32),
        ],
        in_specs=[VMEM],
        out_specs=[VMEM, VMEM],
        compiler_params=kernel_params(),
        name="piece",
    )(parts)


def stacked_kernel(parts_ref, *refs):
    *piece_refs, out_ref = refs
    for block, piece_ref in enumerate(piece_refs):
        out_ref[block] = piece_ref[...]
    out_ref[len(piece_refs)] = jnp.sum(parts_ref[...], axis=0)


def stacked(parts, pieces):
    return pl.pallas_call(
        stacked_kernel,
        out_shape=jax.ShapeDtypeStruct((len(pieces) + 1, *parts.shape[1:]), F32),
        in_specs=[VMEM] * (1 + len(pieces)),
        out_specs=VMEM,
        compiler_params=kernel_params(),
        name="stacked",
    )(parts, *pieces)


def other_core(value):
    peers = lax.axis_size("col")
    return lax.ppermute(value, "col", [(i, i ^ 1) for i in range(peers)])


def total_along_x(value):
    peers = lax.axis_size("col")
    arrived = [
        lax.ppermute(value, "col", [(i, (i + hop) % peers) for i in range(peers)])
        for hop in range(2, peers, 2)
    ]
    for part in arrived:
        value = value + part
    return value


def per_row(value):
    return lax.all_to_all(value, "row", 0, 0, tiled=True)


def per_device(
    sub_field, reluctivity, stride, counts, source_cell, target_row, lower_tiles, diag_inverse
):
    blocks = diag_inverse.shape[0]
    tile_rows = lower_tiles.shape[1]
    rotor = sub_field.shape[1]
    peers = lax.axis_size("row")
    core = (lax.axis_index("col") % 2).astype(jnp.int32).reshape(1)
    picked, targets = pick(
        sub_field, reluctivity, stride, counts, source_cell, target_row[0, 0]
    )
    received = per_row(picked).reshape(-1, rotor)

    shares = []
    pieces = []
    mine, theirs = first_residual(core, targets, received, tile_rows)
    for block in range(blocks):
        mine = total_along_x(mine + other_core(theirs))
        if block + 1 < blocks:
            last = block if block + 2 < blocks else block + 1
            started, lower_high, lower_low, *diags = fold(
                block + 1, block, last, targets, received, lower_tiles, diag_inverse, shares
            )
        diag_high, diag_low, *diags = diags
        partial = diag_product(core, mine, other_core(mine), diag_high, diag_low)
        parts = per_row(partial.reshape(peers, -1, rotor))
        if block + 1 < blocks:
            piece, copies = piece_and_copies(parts)
            pieces.append(piece)
            share = per_row(copies).reshape(-1, rotor)
            shares.append(share)
            mine, theirs = lower_product(core, share, lower_high, lower_low, started)
    return stacked(parts, pieces)[:, None]


def solution(mesh):
    placed = (
        P(("row", "col"), None),
        P(None, ("row", "col"), None),
        P(("row", "col")),
        P(("row", "col"), None),
        P(("row", "col"), None, None),
        P("row", "col", None, None),
        P(None, "row", "col"),
        P(None, "col", "row"),
    )
    return jax.shard_map(
        per_device,
        mesh=mesh,
        in_specs=placed,
        out_specs=P(None, "col", "row", None),
        check_vma=False,
    )
```

```python
import functools

import jax
import jax.numpy as jnp
from jax import lax
from jax.experimental import pallas as pl
from jax.experimental.pallas import tpu as pltpu
from jax.sharding import PartitionSpec as P

F32 = jnp.float32
BF16 = jnp.bfloat16
VMEM_LIMIT = 32 * 1024 * 1024
WIDE_LIMIT = 50 * 1024 * 1024
PICK_LIMIT = 54 * 1024 * 1024
VMEM = pl.BlockSpec(memory_space=pltpu.VMEM)
SMEM = pl.BlockSpec(memory_space=pltpu.SMEM)
HBM = pl.BlockSpec(memory_space=pltpu.HBM)


def kernel_params(limit=VMEM_LIMIT):
    return pltpu.CompilerParams(vmem_limit_bytes=limit)


def dot(left, right):
    return jnp.dot(left, right, preferred_element_type=F32)


def split(value):
    high = value.astype(BF16)
    return high, (value - high.astype(F32)).astype(BF16)


def split_product(left_high, left_low, right):
    width = right.shape[1]
    high, low = split(right)
    both = dot(left_high, jnp.concatenate([high, low], axis=1))
    return both[:, :width] + both[:, width:] + dot(left_low, high)


def pick_kernel(
    core_ref, stride_hbm, counts_hbm, source_hbm, target_ref, field_hbm, nu_hbm,
    out_ref, targets_ref, stride_ref, counts_ref, source_ref, field, nu, sems,
):
    cells = nu.shape[1]
    pad = field.shape[0] - cells
    loads = [
        pltpu.make_async_copy(stride_hbm, stride_ref, sems.at[2]),
        pltpu.make_async_copy(counts_hbm, counts_ref, sems.at[3]),
        pltpu.make_async_copy(source_hbm, source_ref, sems.at[4]),
        pltpu.make_async_copy(field_hbm, field.at[pl.ds(pad, cells)], sems.at[0]),
        pltpu.make_async_copy(nu_hbm, nu, sems.at[1]),
    ]
    for load in loads:
        load.start()
    field[0:pad, :] = jnp.zeros((pad, field.shape[1]), F32)
    width = target_ref.shape[1]
    for sender in range(target_ref.shape[0]):
        targets_ref[0:1, sender * width : (sender + 1) * width] = target_ref[sender : sender + 1, :]
    for load in loads:
        load.wait()
    stride = stride_ref[0]
    slots = source_ref.shape[2]

    @pl.loop(0, source_ref.shape[1])
    def _(grid_row):
        live = counts_ref[0, grid_row]
        for slot in range(slots):
            cell = source_ref[0, grid_row, slot]
            here = field[pl.ds(pad + cell, 1), :]
            radial = here - field[pl.ds(pad + cell - stride, 1), :]
            tangent = here - field[pl.ds(pad - 1 + cell, 1), :]
            swept = nu[0, pl.ds(cell, 1), :] * radial + nu[1, pl.ds(cell, 1), :] * tangent
            out_ref[grid_row, pl.ds(slot, 1), :] = jnp.where(slot < live, swept, 0.0)


def pick(core, sub_field, reluctivity, stride, counts, source_cell, target_row):
    cells, rotor = sub_field.shape
    _, grid_rows, slots = source_cell.shape
    pad = 512
    return pl.pallas_call(
        pick_kernel,
        out_shape=[
            jax.ShapeDtypeStruct((grid_rows, slots, rotor), F32),
            jax.ShapeDtypeStruct((1, target_row.size), jnp.int32),
        ],
        in_specs=[SMEM, HBM, HBM, HBM, VMEM, HBM, HBM],
        out_specs=[VMEM, VMEM],
        scratch_shapes=[
            pltpu.SMEM(stride.shape, jnp.int32),
            pltpu.SMEM(counts.shape, jnp.int32),
            pltpu.SMEM(source_cell.shape, jnp.int32),
            pltpu.VMEM((pad + cells, rotor), F32),
            pltpu.VMEM((2, cells, rotor), F32),
            pltpu.SemaphoreType.DMA((5,)),
        ],
        compiler_params=kernel_params(PICK_LIMIT),
        name="pick",
    )(core, stride, counts, source_cell, target_row, sub_field, reluctivity)


def interface_rows(block, rows, targets_ref, received_ref):
    received = received_ref[...]
    high, low = split(received)
    rest = (received - high.astype(F32) - low.astype(F32)).astype(BF16)
    row = block * rows + lax.broadcasted_iota(jnp.int32, (rows, received.shape[0]), 0)
    chosen = jnp.where(row == targets_ref[...], 1.0, 0.0).astype(BF16)
    both = dot(chosen, jnp.concatenate([high, low], axis=1))
    width = received.shape[1]
    return both[:, :width] + both[:, width:] + dot(chosen, rest)


def halves_out(core_ref, value, mine_ref, theirs_ref, whole):
    whole[...] = value
    half = mine_ref.shape[0]
    core = core_ref[0]
    mine_ref[...] = whole[pl.ds(pl.multiple_of(core * half, half), half), :]
    theirs_ref[...] = whole[pl.ds(pl.multiple_of((1 - core) * half, half), half), :]


def half_shapes(rows, rotor):
    return [jax.ShapeDtypeStruct((rows // 2, rotor), F32)] * 2


def first_kernel(core_ref, targets_ref, received_ref, mine_ref, theirs_ref, whole):
    rows = whole.shape[0]
    value = interface_rows(0, rows, targets_ref, received_ref)
    halves_out(core_ref, value, mine_ref, theirs_ref, whole)


def first_residual(core, targets, received, rows):
    rotor = received.shape[1]
    return pl.pallas_call(
        first_kernel,
        out_shape=half_shapes(rows, rotor),
        in_specs=[SMEM, VMEM, VMEM],
        out_specs=[VMEM, VMEM],
        scratch_shapes=[pltpu.VMEM((rows, rotor), F32)],
        compiler_params=kernel_params(),
        name="first",
    )(core, targets, received)


def fold_kernel(block, first, last, *refs):
    earlier = block - 1
    targets_ref, received_ref, lower_hbm, diag_hbm = refs[:4]
    shares = refs[4 : 4 + earlier]
    outs = refs[4 + earlier : -3]
    tiles, diags, sems = refs[-3:]
    base = block * (block - 1) // 2
    loads = [
        pltpu.make_async_copy(lower_hbm.at[base + j], tiles.at[j], sems.at[j])
        for j in range(block)
    ]
    loads += [
        pltpu.make_async_copy(diag_hbm.at[first + j], diags.at[j], sems.at[block + j])
        for j in range(last - first + 1)
    ]
    for load in loads:
        load.start()
    started_ref, lower_high, lower_low = outs[:3]
    total = interface_rows(block, started_ref.shape[0], targets_ref, received_ref)
    for j in range(earlier):
        loads[j].wait()
        high, low = split(tiles[j])
        total = total - split_product(high, low, shares[j][...])
    started_ref[...] = total
    loads[earlier].wait()
    lower_high[...], lower_low[...] = split(tiles[earlier])
    for j in range(last - first + 1):
        loads[block + j].wait()
        outs[3 + 2 * j][...], outs[4 + 2 * j][...] = split(diags[j])


def fold(block, first, last, targets, received, lower_tiles, diag_inverse, shares):
    _, rows, columns = lower_tiles.shape
    _, out_rows, depth = diag_inverse.shape
    rotor = received.shape[1]
    n_diag = last - first + 1
    shapes = [jax.ShapeDtypeStruct((rows, rotor), F32)]
    shapes += [jax.ShapeDtypeStruct((rows, columns), BF16)] * 2
    shapes += [jax.ShapeDtypeStruct((out_rows, depth), BF16)] * (2 * n_diag)
    return pl.pallas_call(
        functools.partial(fold_kernel, block, first, last),
        out_shape=shapes,
        in_specs=[VMEM, VMEM, HBM, HBM] + [VMEM] * len(shares),
        out_specs=[VMEM] * len(shapes),
        scratch_shapes=[
            pltpu.VMEM((block, rows, columns), F32),
            pltpu.VMEM((n_diag, out_rows, depth), F32),
            pltpu.SemaphoreType.DMA((block + n_diag,)),
        ],
        compiler_params=kernel_params(WIDE_LIMIT),
        cost_estimate=pl.CostEstimate(
            flops=6 * block * rows * columns * rotor,
            bytes_accessed=4 * (block + n_diag) * rows * columns,
            transcendentals=0,
        ),
        name="fold",
    )(targets, received, lower_tiles, diag_inverse, *shares)


def lower_kernel(core_ref, share_ref, high_ref, low_ref, started_ref, mine_ref, theirs_ref, whole):
    value = started_ref[...] - split_product(high_ref[...], low_ref[...], share_ref[...])
    halves_out(core_ref, value, mine_ref, theirs_ref, whole)


def lower_product(core, share, high, low, started):
    rows, rotor = started.shape
    return pl.pallas_call(
        lower_kernel,
        out_shape=half_shapes(rows, rotor),
        in_specs=[SMEM] + [VMEM] * 4,
        out_specs=[VMEM, VMEM],
        scratch_shapes=[pltpu.VMEM((rows, rotor), F32)],
        compiler_params=kernel_params(),
        name="lower",
    )(core, share, high, low, started)


def diag_kernel(core_ref, mine_ref, theirs_ref, high_ref, low_ref, out_ref, whole):
    half = mine_ref.shape[0]
    core = core_ref[0]
    whole[pl.ds(pl.multiple_of(core * half, half), half), :] = mine_ref[...]
    whole[pl.ds(pl.multiple_of((1 - core) * half, half), half), :] = theirs_ref[...]
    out_ref[...] = split_product(high_ref[...], low_ref[...], whole[...])


def diag_product(core, mine, theirs, high, low):
    half, rotor = mine.shape
    return pl.pallas_call(
        diag_kernel,
        out_shape=jax.ShapeDtypeStruct((high.shape[0], rotor), F32),
        in_specs=[SMEM] + [VMEM] * 4,
        out_specs=VMEM,
        scratch_shapes=[pltpu.VMEM((2 * half, rotor), F32)],
        compiler_params=kernel_params(),
        name="diag",
    )(core, mine, theirs, high, low)


def piece_kernel(parts_ref, piece_ref, copies_ref):
    piece = jnp.sum(parts_ref[...], axis=0)
    piece_ref[...] = piece
    for peer in range(copies_ref.shape[0]):
        copies_ref[peer] = piece


def piece_and_copies(parts):
    return pl.pallas_call(
        piece_kernel,
        out_shape=[
            jax.ShapeDtypeStruct(parts.shape[1:], F32),
            jax.ShapeDtypeStruct(parts.shape, F32),
        ],
        in_specs=[VMEM],
        out_specs=[VMEM, VMEM],
        compiler_params=kernel_params(),
        name="piece",
    )(parts)


def stacked_kernel(parts_ref, *refs):
    *piece_refs, out_ref = refs
    for block, piece_ref in enumerate(piece_refs):
        out_ref[block] = piece_ref[...]
    out_ref[len(piece_refs)] = jnp.sum(parts_ref[...], axis=0)


def stacked(parts, pieces):
    return pl.pallas_call(
        stacked_kernel,
        out_shape=jax.ShapeDtypeStruct((len(pieces) + 1, *parts.shape[1:]), F32),
        in_specs=[VMEM] * (1 + len(pieces)),
        out_specs=VMEM,
        compiler_params=kernel_params(),
        name="stacked",
    )(parts, *pieces)


def other_core(value):
    peers = lax.axis_size("col")
    return lax.ppermute(value, "col", [(i, i ^ 1) for i in range(peers)])


def total_along_x(value):
    peers = lax.axis_size("col")
    arrived = [
        lax.ppermute(value, "col", [(i, (i + hop) % peers) for i in range(peers)])
        for hop in range(2, peers, 2)
    ]
    for part in arrived:
        value = value + part
    return value


def per_row(value):
    return lax.all_to_all(value, "row", 0, 0, tiled=True)


def per_device(
    sub_field, reluctivity, stride, counts, source_cell, target_row, lower_tiles, diag_inverse
):
    blocks = diag_inverse.shape[0]
    tile_rows = lower_tiles.shape[1]
    rotor = sub_field.shape[1]
    peers = lax.axis_size("row")
    core = (lax.axis_index("col") % 2).astype(jnp.int32).reshape(1)
    picked, targets = pick(
        core, sub_field, reluctivity, stride, counts, source_cell, target_row[0, 0]
    )
    received = per_row(picked).reshape(-1, rotor)

    shares = []
    pieces = []
    mine, theirs = first_residual(core, targets, received, tile_rows)
    for block in range(blocks):
        mine = total_along_x(mine + other_core(theirs))
        if block + 1 < blocks:
            last = block if block + 2 < blocks else block + 1
            folded = fold(
                block + 1, block, last, targets, received, lower_tiles, diag_inverse, shares
            )
            mine, (started, lower_high, lower_low, *diags) = lax.optimization_barrier(
                (mine, folded)
            )
        diag_high, diag_low, *diags = diags
        partial = diag_product(core, mine, other_core(mine), diag_high, diag_low)
        parts = per_row(partial.reshape(peers, -1, rotor))
        if block + 1 < blocks:
            piece, copies = piece_and_copies(parts)
            pieces.append(piece)
            share = per_row(copies).reshape(-1, rotor)
            shares.append(share)
            mine, theirs = lower_product(core, share, lower_high, lower_low, started)
    return stacked(parts, pieces)[:, None]


def solution(mesh):
    placed = (
        P(("row", "col"), None),
        P(None, ("row", "col"), None),
        P(("row", "col")),
        P(("row", "col"), None),
        P(("row", "col"), None, None),
        P("row", "col", None, None),
        P(None, "row", "col"),
        P(None, "col", "row"),
    )
    return jax.shard_map(
        per_device,
        mesh=mesh,
        in_specs=placed,
        out_specs=P(None, "col", "row", None),
        check_vma=False,
    )
```

```python
import functools

import jax
import jax.numpy as jnp
from jax import lax
from jax.experimental import pallas as pl
from jax.experimental.pallas import tpu as pltpu
from jax.sharding import PartitionSpec as P

F32 = jnp.float32
BF16 = jnp.bfloat16
VMEM_LIMIT = 32 * 1024 * 1024
WIDE_LIMIT = 50 * 1024 * 1024
PICK_LIMIT = 54 * 1024 * 1024
VMEM = pl.BlockSpec(memory_space=pltpu.VMEM)
SMEM = pl.BlockSpec(memory_space=pltpu.SMEM)
HBM = pl.BlockSpec(memory_space=pltpu.HBM)


def kernel_params(limit=VMEM_LIMIT):
    return pltpu.CompilerParams(vmem_limit_bytes=limit)


def dot(left, right):
    return jnp.dot(left, right, preferred_element_type=F32)


def split(value):
    high = value.astype(BF16)
    return high, (value - high.astype(F32)).astype(BF16)


def split_product(left_high, left_low, right):
    width = right.shape[1]
    high, low = split(right)
    both = dot(left_high, jnp.concatenate([high, low], axis=1))
    return both[:, :width] + both[:, width:] + dot(left_low, high)


def pick_kernel(
    core_ref, stride_hbm, counts_hbm, source_hbm, target_ref, field_hbm, nu_hbm,
    out_ref, targets_ref, stride_ref, counts_ref, source_ref, field, nu, sems,
):
    cells = nu.shape[1]
    pad = field.shape[0] - cells
    loads = [
        pltpu.make_async_copy(stride_hbm, stride_ref, sems.at[2]),
        pltpu.make_async_copy(counts_hbm, counts_ref, sems.at[3]),
        pltpu.make_async_copy(source_hbm, source_ref, sems.at[4]),
        pltpu.make_async_copy(field_hbm, field.at[pl.ds(pad, cells)], sems.at[0]),
        pltpu.make_async_copy(nu_hbm, nu, sems.at[1]),
    ]
    for load in loads:
        load.start()
    field[0:pad, :] = jnp.zeros((pad, field.shape[1]), F32)
    width = target_ref.shape[1]
    for sender in range(target_ref.shape[0]):
        targets_ref[0:1, sender * width : (sender + 1) * width] = target_ref[sender : sender + 1, :]
    for load in loads:
        load.wait()
    stride = stride_ref[0]
    slots = source_ref.shape[2]

    @pl.loop(0, source_ref.shape[1])
    def _(grid_row):
        live = counts_ref[0, grid_row]
        for slot in range(slots):
            cell = source_ref[0, grid_row, slot]
            here = field[pl.ds(pad + cell, 1), :]
            radial = here - field[pl.ds(pad + cell - stride, 1), :]
            tangent = here - field[pl.ds(pad - 1 + cell, 1), :]
            swept = nu[0, pl.ds(cell, 1), :] * radial + nu[1, pl.ds(cell, 1), :] * tangent
            out_ref[grid_row, pl.ds(slot, 1), :] = jnp.where(slot < live, swept, 0.0)


def pick(core, sub_field, reluctivity, stride, counts, source_cell, target_row):
    cells, rotor = sub_field.shape
    _, grid_rows, slots = source_cell.shape
    pad = 512
    return pl.pallas_call(
        pick_kernel,
        out_shape=[
            jax.ShapeDtypeStruct((grid_rows, slots, rotor), F32),
            jax.ShapeDtypeStruct((1, target_row.size), jnp.int32),
        ],
        in_specs=[SMEM, HBM, HBM, HBM, VMEM, HBM, HBM],
        out_specs=[VMEM, VMEM],
        scratch_shapes=[
            pltpu.SMEM(stride.shape, jnp.int32),
            pltpu.SMEM(counts.shape, jnp.int32),
            pltpu.SMEM(source_cell.shape, jnp.int32),
            pltpu.VMEM((pad + cells, rotor), F32),
            pltpu.VMEM((2, cells, rotor), F32),
            pltpu.SemaphoreType.DMA((5,)),
        ],
        compiler_params=kernel_params(PICK_LIMIT),
        name="pick",
    )(core, stride, counts, source_cell, target_row, sub_field, reluctivity)


def left_lanes(shape):
    return lax.broadcasted_iota(jnp.int32, shape, 1) < shape[1] // 2


def swap_lanes(value):
    return pltpu.roll(value, value.shape[1] // 2, 1)


def packed(own, other):
    half = own.shape[0] // 2
    return jnp.where(
        left_lanes((half, own.shape[1])),
        own[:half] + swap_lanes(other[:half]),
        swap_lanes(own[half:]) + other[half:],
    )


def three_parts(value):
    high, low = split(value)
    rest = (value - high.astype(F32) - low.astype(F32)).astype(BF16)
    return jnp.concatenate([high, low], axis=1), rest


def interface_rows(block, rows, targets_ref, parts):
    pair, rest = parts
    width = rest.shape[1]
    row = block * rows + lax.broadcasted_iota(jnp.int32, (rows, rest.shape[0]), 0)
    chosen = jnp.where(row == targets_ref[...], 1.0, 0.0).astype(BF16)
    both = dot(chosen, pair)
    return both[:, :width] + both[:, width:] + dot(chosen, rest)


def first_kernel(rows, core_ref, own_ref, other_ref, received_ref, swapped_ref, out_ref, slots_ref):
    received, swapped = received_ref[...], swapped_ref[...]
    left = left_lanes(received.shape)
    low = jnp.where(left, received, swap_lanes(swapped))
    high = jnp.where(left, swap_lanes(received), swapped)
    slots = jnp.where(core_ref[0] == 0, low, high)
    slots_ref[...] = slots
    parts = three_parts(slots)
    out_ref[...] = packed(
        interface_rows(0, rows, own_ref, parts), interface_rows(0, rows, other_ref, parts)
    )


def first_residual(core, own_targets, other_targets, received, swapped, rows):
    rotor = received.shape[1]
    return pl.pallas_call(
        functools.partial(first_kernel, rows),
        out_shape=[
            jax.ShapeDtypeStruct((rows // 2, rotor), F32),
            jax.ShapeDtypeStruct(received.shape, F32),
        ],
        in_specs=[SMEM] + [VMEM] * 4,
        out_specs=[VMEM, VMEM],
        compiler_params=kernel_params(),
        name="first",
    )(core, own_targets, other_targets, received, swapped)


def fold_kernel(block, *refs):
    earlier = block - 1
    own_targets, other_targets, slots_ref, *hbm = refs[:7]
    shares = refs[7 : 7 + earlier]
    started_ref, *outs = refs[7 + earlier : -3]
    tiles, diags, sems = refs[-3:]
    base = block * (block - 1) // 2
    loads = []
    for j in range(block):
        for side in range(2):
            at = 2 * j + side
            loads.append(pltpu.make_async_copy(hbm[side].at[base + j], tiles.at[at], sems.at[at]))
    for side in range(2):
        loads.append(
            pltpu.make_async_copy(
                hbm[2 + side].at[earlier], diags.at[side], sems.at[2 * block + side]
            )
        )
    for load in loads:
        load.start()
    parts = three_parts(slots_ref[...])
    rows = tiles.shape[1]
    totals = [
        interface_rows(block, rows, targets, parts) for targets in (own_targets, other_targets)
    ]
    for j in range(earlier):
        share = shares[j][...]
        for side in range(2):
            loads[2 * j + side].wait()
            high, low = split(tiles[2 * j + side])
            totals[side] = totals[side] - split_product(high, low, share)
    started_ref[...] = packed(*totals)
    for side in range(2):
        loads[2 * earlier + side].wait()
        outs[2 * side][...], outs[2 * side + 1][...] = split(tiles[2 * earlier + side])
    for side in range(2):
        loads[2 * block + side].wait()
        outs[4 + 2 * side][...], outs[5 + 2 * side][...] = split(diags[side])


def fold(block, own_targets, other_targets, slots, lowers, diags, shares):
    _, rows, columns = lowers[0].shape
    _, out_rows, depth = diags[0].shape
    rotor = slots.shape[1]
    shapes = [jax.ShapeDtypeStruct((rows // 2, rotor), F32)]
    shapes += [jax.ShapeDtypeStruct((rows, columns), BF16)] * 4
    shapes += [jax.ShapeDtypeStruct((out_rows, depth), BF16)] * 4
    return pl.pallas_call(
        functools.partial(fold_kernel, block),
        out_shape=shapes,
        in_specs=[VMEM] * 3 + [HBM] * 4 + [VMEM] * len(shares),
        out_specs=[VMEM] * len(shapes),
        scratch_shapes=[
            pltpu.VMEM((2 * block, rows, columns), F32),
            pltpu.VMEM((2, out_rows, depth), F32),
            pltpu.SemaphoreType.DMA((2 * block + 2,)),
        ],
        compiler_params=kernel_params(WIDE_LIMIT),
        cost_estimate=pl.CostEstimate(
            flops=12 * block * rows * columns * rotor,
            bytes_accessed=8 * (block + 1) * rows * columns,
            transcendentals=0,
        ),
        name="fold",
    )(own_targets, other_targets, slots, *lowers, *diags, *shares)


def prepare_kernel(block, own_hbm, other_hbm, *refs):
    *outs, diags, sems = refs
    loads = [
        pltpu.make_async_copy(hbm.at[block], diags.at[side], sems.at[side])
        for side, hbm in enumerate((own_hbm, other_hbm))
    ]
    for load in loads:
        load.start()
    for side in range(2):
        loads[side].wait()
        outs[2 * side][...], outs[2 * side + 1][...] = split(diags[side])


def prepare(block, diags):
    _, out_rows, depth = diags[0].shape
    return pl.pallas_call(
        functools.partial(prepare_kernel, block),
        out_shape=[jax.ShapeDtypeStruct((out_rows, depth), BF16)] * 4,
        in_specs=[HBM] * 2,
        out_specs=[VMEM] * 4,
        scratch_shapes=[
            pltpu.VMEM((2, out_rows, depth), F32),
            pltpu.SemaphoreType.DMA((2,)),
        ],
        compiler_params=kernel_params(WIDE_LIMIT),
        cost_estimate=pl.CostEstimate(
            flops=8 * out_rows * depth,
            bytes_accessed=16 * out_rows * depth,
            transcendentals=0,
        ),
        name="prepare",
    )(*diags)


def lower_kernel(share_ref, own_high, own_low, other_high, other_low, started_ref, out_ref):
    share = share_ref[...]
    out_ref[...] = started_ref[...] - packed(
        split_product(own_high[...], own_low[...], share),
        split_product(other_high[...], other_low[...], share),
    )


def lower_product(share, tiles, started):
    return pl.pallas_call(
        lower_kernel,
        out_shape=jax.ShapeDtypeStruct(started.shape, F32),
        in_specs=[VMEM] * 6,
        out_specs=VMEM,
        compiler_params=kernel_params(),
        name="lower",
    )(share, *tiles, started)


def diag_kernel(*refs):
    *residual_refs, own_high, own_low, other_high, other_low, out_ref = refs
    residual = residual_refs[0][...]
    for ref in residual_refs[1:]:
        residual = residual + ref[...]
    turned = swap_lanes(residual)
    left = left_lanes(residual.shape)
    on_left = jnp.concatenate(
        [jnp.where(left, residual, 0.0), jnp.where(left, turned, 0.0)], axis=0
    )
    on_right = jnp.concatenate(
        [jnp.where(left, 0.0, turned), jnp.where(left, 0.0, residual)], axis=0
    )
    out_ref[...] = split_product(own_high[...], own_low[...], on_left) + split_product(
        other_high[...], other_low[...], on_right
    )


def diag_product(residuals, tiles):
    return pl.pallas_call(
        diag_kernel,
        out_shape=jax.ShapeDtypeStruct((tiles[0].shape[0], residuals[0].shape[1]), F32),
        in_specs=[VMEM] * (len(residuals) + 4),
        out_specs=VMEM,
        compiler_params=kernel_params(),
        name="diag",
    )(*residuals, *tiles)


def piece_kernel(parts_ref, piece_ref, copies_ref):
    piece = jnp.sum(parts_ref[...], axis=0)
    piece_ref[...] = piece
    for peer in range(copies_ref.shape[0]):
        copies_ref[peer] = piece


def piece_and_copies(parts):
    return pl.pallas_call(
        piece_kernel,
        out_shape=[
            jax.ShapeDtypeStruct(parts.shape[1:], F32),
            jax.ShapeDtypeStruct(parts.shape, F32),
        ],
        in_specs=[VMEM],
        out_specs=[VMEM, VMEM],
        compiler_params=kernel_params(),
        name="piece",
    )(parts)


def join_kernel(*refs):
    *piece_refs, out_ref = refs
    for block, piece_ref in enumerate(piece_refs):
        out_ref[block] = piece_ref[...]


def joined(pieces):
    return pl.pallas_call(
        join_kernel,
        out_shape=jax.ShapeDtypeStruct((len(pieces), *pieces[0].shape), F32),
        in_specs=[VMEM] * len(pieces),
        out_specs=VMEM,
        compiler_params=kernel_params(),
        name="join",
    )(*pieces)


def stacked_kernel(core_ref, early_ref, early_other_ref, last_ref, last_other_ref, out_ref):
    left = left_lanes(last_ref.shape)
    first_core = core_ref[0] == 0
    early = early_ref.shape[0]
    for block in range(early + 1):
        own = early_ref[block] if block < early else last_ref[...]
        other = early_other_ref[block] if block < early else last_other_ref[...]
        rows = jnp.where(left, own, other)
        out_ref[block] = jnp.where(first_core, rows, swap_lanes(rows))


def stacked(core, early, early_other, last, last_other):
    return pl.pallas_call(
        stacked_kernel,
        out_shape=jax.ShapeDtypeStruct((early.shape[0] + 1, *last.shape), F32),
        in_specs=[SMEM] + [VMEM] * 4,
        out_specs=VMEM,
        compiler_params=kernel_params(),
        name="stacked",
    )(core, early, early_other, last, last_other)


def other_core(value):
    peers = lax.axis_size("col")
    return lax.ppermute(value, "col", [(i, i ^ 1) for i in range(peers)])


def along_x(value):
    peers = lax.axis_size("col")
    return [value] + [
        lax.ppermute(value, "col", [(i, i ^ apart) for i in range(peers)])
        for apart in (2, 6, 4)
    ]


def per_row(value):
    return lax.all_to_all(value, "row", 0, 0, tiled=True)


def per_device(
    sub_field, reluctivity, stride, counts, source_cell, target_row, lower_tiles, diag_inverse
):
    blocks = diag_inverse.shape[0]
    tile_rows = lower_tiles.shape[1]
    rotor = sub_field.shape[1]
    peers = lax.axis_size("row")
    core = (lax.axis_index("col") % 2).astype(jnp.int32).reshape(1)
    diags = (diag_inverse, other_core(diag_inverse))
    lowers = (lower_tiles, other_core(lower_tiles))
    picked, targets = pick(
        core, sub_field, reluctivity, stride, counts, source_cell, target_row[0, 0]
    )
    other_targets = other_core(targets)
    received = per_row(picked).reshape(-1, rotor)

    shares = []
    pieces = []
    residual, slots = first_residual(
        core, targets, other_targets, received, other_core(received), tile_rows
    )
    for block in range(blocks):
        residuals = along_x(residual)
        if block + 1 < blocks:
            started, *tiles = fold(
                block + 1, targets, other_targets, slots, lowers, diags, shares
            )
            tiles, diag_tiles = tiles[:4], tiles[4:]
        else:
            diag_tiles = prepare(block, diags)
            early = joined(pieces)
            early_other = other_core(early)
        parts = per_row(diag_product(residuals, diag_tiles).reshape(peers, -1, rotor))
        if block + 1 < blocks:
            piece, copies = piece_and_copies(parts)
            pieces.append(piece)
            share = per_row(copies).reshape(-1, rotor)
            shares.append(share)
            residual = lower_product(share, tiles, started)
    last = jnp.sum(parts, axis=0)
    return stacked(core, early, early_other, last, other_core(last))[:, None]


def solution(mesh):
    placed = (
        P(("row", "col"), None),
        P(None, ("row", "col"), None),
        P(("row", "col")),
        P(("row", "col"), None),
        P(("row", "col"), None, None),
        P("row", "col", None, None),
        P(None, "row", "col"),
        P(None, "col", "row"),
    )
    return jax.shard_map(
        per_device,
        mesh=mesh,
        in_specs=placed,
        out_specs=P(None, "col", "row", None),
        check_vma=False,
    )
```

```python
import functools

import jax
import jax.numpy as jnp
from jax import lax
from jax.experimental import pallas as pl
from jax.experimental.pallas import tpu as pltpu
from jax.sharding import PartitionSpec as P

F32 = jnp.float32
BF16 = jnp.bfloat16
VMEM_LIMIT = 32 * 1024 * 1024
WIDE_LIMIT = 50 * 1024 * 1024
PICK_LIMIT = 54 * 1024 * 1024
VMEM = pl.BlockSpec(memory_space=pltpu.VMEM)
SMEM = pl.BlockSpec(memory_space=pltpu.SMEM)
HBM = pl.BlockSpec(memory_space=pltpu.HBM)


def kernel_params(limit=VMEM_LIMIT):
    return pltpu.CompilerParams(vmem_limit_bytes=limit)


def dot(left, right):
    return jnp.dot(left, right, preferred_element_type=F32)


def split(value):
    high = value.astype(BF16)
    return high, (value - high.astype(F32)).astype(BF16)


def split_product(left_high, left_low, right):
    width = right.shape[1]
    high, low = split(right)
    both = dot(left_high, jnp.concatenate([high, low], axis=1))
    return both[:, :width] + both[:, width:] + dot(left_low, high)


def pick_kernel(
    core_ref, stride_hbm, counts_hbm, source_hbm, target_ref, field_hbm, nu_hbm,
    out_ref, targets_ref, stride_ref, counts_ref, source_ref, field, nu, sems,
):
    cells = nu.shape[1]
    pad = field.shape[0] - cells
    loads = [
        pltpu.make_async_copy(stride_hbm, stride_ref, sems.at[2]),
        pltpu.make_async_copy(counts_hbm, counts_ref, sems.at[3]),
        pltpu.make_async_copy(source_hbm, source_ref, sems.at[4]),
        pltpu.make_async_copy(field_hbm, field.at[pl.ds(pad, cells)], sems.at[0]),
        pltpu.make_async_copy(nu_hbm, nu, sems.at[1]),
    ]
    for load in loads:
        load.start()
    field[0:pad, :] = jnp.zeros((pad, field.shape[1]), F32)
    width = target_ref.shape[1]
    for sender in range(target_ref.shape[0]):
        targets_ref[0:1, sender * width : (sender + 1) * width] = target_ref[sender : sender + 1, :]
    for load in loads:
        load.wait()
    stride = stride_ref[0]
    slots = source_ref.shape[2]

    @pl.loop(0, source_ref.shape[1])
    def _(grid_row):
        live = counts_ref[0, grid_row]
        for slot in range(slots):
            cell = source_ref[0, grid_row, slot]
            here = field[pl.ds(pad + cell, 1), :]
            radial = here - field[pl.ds(pad + cell - stride, 1), :]
            tangent = here - field[pl.ds(pad - 1 + cell, 1), :]
            swept = nu[0, pl.ds(cell, 1), :] * radial + nu[1, pl.ds(cell, 1), :] * tangent
            out_ref[grid_row, pl.ds(slot, 1), :] = jnp.where(slot < live, swept, 0.0)


def pick(core, sub_field, reluctivity, stride, counts, source_cell, target_row):
    cells, rotor = sub_field.shape
    _, grid_rows, slots = source_cell.shape
    pad = 512
    return pl.pallas_call(
        pick_kernel,
        out_shape=[
            jax.ShapeDtypeStruct((grid_rows, slots, rotor), F32),
            jax.ShapeDtypeStruct((1, target_row.size), jnp.int32),
        ],
        in_specs=[SMEM, HBM, HBM, HBM, VMEM, HBM, HBM],
        out_specs=[VMEM, VMEM],
        scratch_shapes=[
            pltpu.SMEM(stride.shape, jnp.int32),
            pltpu.SMEM(counts.shape, jnp.int32),
            pltpu.SMEM(source_cell.shape, jnp.int32),
            pltpu.VMEM((pad + cells, rotor), F32),
            pltpu.VMEM((2, cells, rotor), F32),
            pltpu.SemaphoreType.DMA((5,)),
        ],
        compiler_params=kernel_params(PICK_LIMIT),
        name="pick",
    )(core, stride, counts, source_cell, target_row, sub_field, reluctivity)


def left_lanes(shape):
    return lax.broadcasted_iota(jnp.int32, shape, 1) < shape[1] // 2


def swap_lanes(value):
    return pltpu.roll(value, value.shape[1] // 2, 1)


def packed(own, other):
    half = own.shape[0] // 2
    return jnp.where(
        left_lanes((half, own.shape[1])),
        own[:half] + swap_lanes(other[:half]),
        swap_lanes(own[half:]) + other[half:],
    )


def three_parts(value):
    high, low = split(value)
    rest = (value - high.astype(F32) - low.astype(F32)).astype(BF16)
    return jnp.concatenate([high, low], axis=1), rest


def interface_rows(block, rows, targets, parts):
    pair, rest = parts
    width = rest.shape[1]
    row = block * rows + lax.broadcasted_iota(jnp.int32, (rows, rest.shape[0]), 0)
    chosen = jnp.where(row == targets, 1.0, 0.0).astype(BF16)
    both = dot(chosen, pair)
    return both[:, :width] + both[:, width:] + dot(chosen, rest)


def fill_interface(block, targets_ref, slots, totals):
    pair, rest = three_parts(slots)

    @pl.loop(0, 2)
    def _(side):
        totals[side] = interface_rows(block, totals.shape[1], targets_ref[side], (pair, rest))


def first_kernel(
    core_ref, own_ref, other_ref, received_ref, swapped_ref, out_ref, slots_ref, targets_ref, totals
):
    targets_ref[0] = own_ref[...]
    targets_ref[1] = other_ref[...]
    received, swapped = received_ref[...], swapped_ref[...]
    left = left_lanes(received.shape)
    low = jnp.where(left, received, swap_lanes(swapped))
    high = jnp.where(left, swap_lanes(received), swapped)
    slots = jnp.where(core_ref[0] == 0, low, high)
    slots_ref[...] = slots
    fill_interface(0, targets_ref, slots, totals)
    out_ref[...] = packed(totals[0], totals[1])


def first_residual(core, own_targets, other_targets, received, swapped, rows):
    rotor = received.shape[1]
    return pl.pallas_call(
        first_kernel,
        out_shape=[
            jax.ShapeDtypeStruct((rows // 2, rotor), F32),
            jax.ShapeDtypeStruct(received.shape, F32),
            jax.ShapeDtypeStruct((2, *own_targets.shape), jnp.int32),
        ],
        in_specs=[SMEM] + [VMEM] * 4,
        out_specs=[VMEM] * 3,
        scratch_shapes=[pltpu.VMEM((2, rows, rotor), F32)],
        compiler_params=kernel_params(),
        name="first",
    )(core, own_targets, other_targets, received, swapped)


def split_sides(load, tiles, first, high_ref, low_ref):
    @pl.loop(0, 2)
    def _(side):
        load(first + side).wait()
        high_ref[side], low_ref[side] = split(tiles[first + side])


def fold_kernel(block, with_diag, *refs):
    earlier = block - 1
    refs = list(refs)
    targets_ref, slots_ref = refs[:2]
    lowers = refs[2:4]
    diags = refs[4:6] if with_diag else []
    at = 4 + len(diags)
    shares = refs[at : at + earlier]
    at += earlier
    started_ref, lower_high, lower_low = refs[at : at + 3]
    at += 3
    diag_outs = refs[at : at + 2] if with_diag else []
    at += len(diag_outs)
    totals, tiles, held, sems, share_sems = refs[at : at + 5]
    base = block * (block - 1) // 2

    for j in range(block):
        for side in range(2):
            at_tile = 2 * j + side
            pltpu.make_async_copy(
                lowers[side].at[base + j], tiles.at[at_tile], sems.at[at_tile]
            ).start()
    for j in range(earlier):
        pltpu.make_async_copy(shares[j], held.at[j], share_sems.at[j]).start()

    def loaded(at_tile):
        return pltpu.make_async_copy(lowers[0].at[0], tiles.at[at_tile], sems.at[at_tile])

    if with_diag:
        diag_tiles, diag_sems = refs[-2:]

        def diag_loaded(side):
            return pltpu.make_async_copy(diags[0].at[0], diag_tiles.at[side], diag_sems.at[side])

        for side in range(2):
            pltpu.make_async_copy(
                diags[side].at[earlier], diag_tiles.at[side], diag_sems.at[side]
            ).start()

    fill_interface(block, targets_ref, slots_ref[...], totals)
    for j in range(earlier):
        pltpu.make_async_copy(shares[j], held.at[j], share_sems.at[j]).wait()
    if earlier:

        @pl.loop(0, 2 * earlier)
        def _(at_tile):
            loaded(at_tile).wait()
            high, low = split(tiles[at_tile])
            side = lax.rem(at_tile, 2)
            totals[side] = totals[side] - split_product(high, low, held[lax.div(at_tile, 2)])

    started_ref[...] = packed(totals[0], totals[1])
    split_sides(loaded, tiles, 2 * earlier, lower_high, lower_low)
    if with_diag:
        split_sides(diag_loaded, diag_tiles, 0, *diag_outs)


def fold(block, targets, slots, lowers, diags, shares):
    _, rows, columns = lowers[0].shape
    rotor = slots.shape[1]
    shapes = [jax.ShapeDtypeStruct((rows // 2, rotor), F32)]
    shapes += [jax.ShapeDtypeStruct((2, rows, columns), BF16)] * 2
    scratch = [
        pltpu.VMEM((2, rows, rotor), F32),
        pltpu.VMEM((2 * block, rows, columns), F32),
        pltpu.VMEM((max(block - 1, 1), columns, rotor), F32),
        pltpu.SemaphoreType.DMA((2 * block,)),
        pltpu.SemaphoreType.DMA((block,)),
    ]
    if diags:
        _, out_rows, depth = diags[0].shape
        shapes += [jax.ShapeDtypeStruct((2, out_rows, depth), BF16)] * 2
        scratch += [pltpu.VMEM((2, out_rows, depth), F32), pltpu.SemaphoreType.DMA((2,))]
    return pl.pallas_call(
        functools.partial(fold_kernel, block, bool(diags)),
        out_shape=shapes,
        in_specs=[VMEM] * 2 + [HBM] * (2 + len(diags)) + [VMEM] * len(shares),
        out_specs=[VMEM] * len(shapes),
        scratch_shapes=scratch,
        compiler_params=kernel_params(WIDE_LIMIT),
        cost_estimate=pl.CostEstimate(
            flops=12 * block * rows * columns * rotor,
            bytes_accessed=8 * (block + 1) * rows * columns,
            transcendentals=0,
        ),
        name="fold",
    )(targets, slots, *lowers, *diags, *shares)


def prepare_kernel(block, own_hbm, other_hbm, high_ref, low_ref, diags, sems):
    for side, hbm in enumerate((own_hbm, other_hbm)):
        pltpu.make_async_copy(hbm.at[block], diags.at[side], sems.at[side]).start()

    def loaded(side):
        return pltpu.make_async_copy(own_hbm.at[block], diags.at[side], sems.at[side])

    split_sides(loaded, diags, 0, high_ref, low_ref)


def prepare(block, diags):
    _, out_rows, depth = diags[0].shape
    return pl.pallas_call(
        functools.partial(prepare_kernel, block),
        out_shape=[jax.ShapeDtypeStruct((2, out_rows, depth), BF16)] * 2,
        in_specs=[HBM] * 2,
        out_specs=[VMEM] * 2,
        scratch_shapes=[
            pltpu.VMEM((2, out_rows, depth), F32),
            pltpu.SemaphoreType.DMA((2,)),
        ],
        compiler_params=kernel_params(WIDE_LIMIT),
        cost_estimate=pl.CostEstimate(
            flops=8 * out_rows * depth,
            bytes_accessed=16 * out_rows * depth,
            transcendentals=0,
        ),
        name="prepare",
    )(*diags)


def lower_kernel(share_ref, high_ref, low_ref, started_ref, out_ref):
    share = share_ref[...]
    out_ref[...] = started_ref[...] - packed(
        split_product(high_ref[0], low_ref[0], share), split_product(high_ref[1], low_ref[1], share)
    )


def lower_product(share, tiles, started):
    return pl.pallas_call(
        lower_kernel,
        out_shape=jax.ShapeDtypeStruct(started.shape, F32),
        in_specs=[VMEM] * 4,
        out_specs=VMEM,
        compiler_params=kernel_params(),
        name="lower",
    )(share, *tiles, started)


def diag_kernel(*refs):
    *residual_refs, high_ref, low_ref, out_ref = refs
    residual = residual_refs[0][...]
    for ref in residual_refs[1:]:
        residual = residual + ref[...]
    turned = swap_lanes(residual)
    left = left_lanes(residual.shape)
    on_left = jnp.concatenate(
        [jnp.where(left, residual, 0.0), jnp.where(left, turned, 0.0)], axis=0
    )
    on_right = jnp.concatenate(
        [jnp.where(left, 0.0, turned), jnp.where(left, 0.0, residual)], axis=0
    )
    out_ref[...] = split_product(high_ref[0], low_ref[0], on_left) + split_product(
        high_ref[1], low_ref[1], on_right
    )


def diag_product(residuals, tiles):
    return pl.pallas_call(
        diag_kernel,
        out_shape=jax.ShapeDtypeStruct((tiles[0].shape[1], residuals[0].shape[1]), F32),
        in_specs=[VMEM] * (len(residuals) + 2),
        out_specs=VMEM,
        compiler_params=kernel_params(),
        name="diag",
    )(*residuals, *tiles)


def piece_kernel(parts_ref, piece_ref, copies_ref):
    piece = jnp.sum(parts_ref[...], axis=0)
    piece_ref[...] = piece
    for peer in range(copies_ref.shape[0]):
        copies_ref[peer] = piece


def piece_and_copies(parts):
    return pl.pallas_call(
        piece_kernel,
        out_shape=[
            jax.ShapeDtypeStruct(parts.shape[1:], F32),
            jax.ShapeDtypeStruct(parts.shape, F32),
        ],
        in_specs=[VMEM],
        out_specs=[VMEM, VMEM],
        compiler_params=kernel_params(),
        name="piece",
    )(parts)


def join_kernel(*refs):
    *piece_refs, out_ref = refs
    for block, piece_ref in enumerate(piece_refs):
        out_ref[block] = piece_ref[...]


def joined(pieces):
    return pl.pallas_call(
        join_kernel,
        out_shape=jax.ShapeDtypeStruct((len(pieces), *pieces[0].shape), F32),
        in_specs=[VMEM] * len(pieces),
        out_specs=VMEM,
        compiler_params=kernel_params(),
        name="join",
    )(*pieces)


def stacked_kernel(core_ref, early_ref, early_other_ref, last_ref, last_other_ref, out_ref):
    left = left_lanes(last_ref.shape)
    first_core = core_ref[0] == 0
    early = early_ref.shape[0]
    for block in range(early + 1):
        own = early_ref[block] if block < early else last_ref[...]
        other = early_other_ref[block] if block < early else last_other_ref[...]
        rows = jnp.where(left, own, other)
        out_ref[block] = jnp.where(first_core, rows, swap_lanes(rows))


def stacked(core, early, early_other, last, last_other):
    return pl.pallas_call(
        stacked_kernel,
        out_shape=jax.ShapeDtypeStruct((early.shape[0] + 1, *last.shape), F32),
        in_specs=[SMEM] + [VMEM] * 4,
        out_specs=VMEM,
        compiler_params=kernel_params(),
        name="stacked",
    )(core, early, early_other, last, last_other)


def other_core(value):
    peers = lax.axis_size("col")
    return lax.ppermute(value, "col", [(i, i ^ 1) for i in range(peers)])


def along_x(value):
    peers = lax.axis_size("col")
    return [value] + [
        lax.ppermute(value, "col", [(i, i ^ apart) for i in range(peers)])
        for apart in (2, 6, 4)
    ]


def per_row(value):
    return lax.all_to_all(value, "row", 0, 0, tiled=True)


def per_device(
    sub_field, reluctivity, stride, counts, source_cell, target_row, lower_tiles, diag_inverse
):
    blocks = diag_inverse.shape[0]
    tile_rows = lower_tiles.shape[1]
    rotor = sub_field.shape[1]
    peers = lax.axis_size("row")
    core = (lax.axis_index("col") % 2).astype(jnp.int32).reshape(1)
    diags = (diag_inverse, other_core(diag_inverse))
    picked, targets = pick(
        core, sub_field, reluctivity, stride, counts, source_cell, target_row[0, 0]
    )
    other_targets = other_core(targets)
    received = per_row(picked).reshape(-1, rotor)

    shares = []
    pieces = []
    residual, slots, targets = first_residual(
        core, targets, other_targets, received, other_core(received), tile_rows
    )
    own_lower, slots = lax.optimization_barrier((lower_tiles, slots))
    lowers = (lower_tiles, other_core(own_lower))
    for block in range(blocks):
        later = block + 1
        if later == blocks:
            residual, pieces = lax.optimization_barrier((residual, pieces))
        residuals = along_x(residual)
        if later < blocks:
            started, lower_high, lower_low, *diag_tiles = fold(
                later, targets, slots, lowers, diags if block else (), shares
            )
        if block == 0 or later == blocks:
            diag_tiles = prepare(block, diags)
        if later == blocks:
            early = joined(pieces)
            diag_tiles, early, early_other = lax.optimization_barrier(
                (diag_tiles, early, other_core(early))
            )
        parts = per_row(diag_product(residuals, diag_tiles).reshape(peers, -1, rotor))
        if later < blocks:
            piece, copies = piece_and_copies(parts)
            pieces.append(piece)
            share = per_row(copies).reshape(-1, rotor)
            shares.append(share)
            residual = lower_product(share, (lower_high, lower_low), started)
    last = jnp.sum(parts, axis=0)
    return stacked(core, early, early_other, last, other_core(last))[:, None]


def solution(mesh):
    placed = (
        P(("row", "col"), None),
        P(None, ("row", "col"), None),
        P(("row", "col")),
        P(("row", "col"), None),
        P(("row", "col"), None, None),
        P("row", "col", None, None),
        P(None, "row", "col"),
        P(None, "col", "row"),
    )
    return jax.shard_map(
        per_device,
        mesh=mesh,
        in_specs=placed,
        out_specs=P(None, "col", "row", None),
        check_vma=False,
    )
```

```python
import functools

import jax
import jax.numpy as jnp
from jax import lax
from jax.experimental import pallas as pl
from jax.experimental.pallas import tpu as pltpu
from jax.sharding import PartitionSpec as P

F32 = jnp.float32
BF16 = jnp.bfloat16
VMEM_LIMIT = 32 * 1024 * 1024
WIDE_LIMIT = 50 * 1024 * 1024
PICK_LIMIT = 54 * 1024 * 1024
VMEM = pl.BlockSpec(memory_space=pltpu.VMEM)
SMEM = pl.BlockSpec(memory_space=pltpu.SMEM)
HBM = pl.BlockSpec(memory_space=pltpu.HBM)


def kernel_params(limit=VMEM_LIMIT):
    return pltpu.CompilerParams(vmem_limit_bytes=limit)


def dot(left, right):
    return jnp.dot(left, right, preferred_element_type=F32)


def split(value):
    high = value.astype(BF16)
    return high, (value - high.astype(F32)).astype(BF16)


def split_product(left_high, left_low, right):
    width = right.shape[1]
    high, low = split(right)
    both = dot(left_high, jnp.concatenate([high, low], axis=1))
    return both[:, :width] + both[:, width:] + dot(left_low, high)


def pick_kernel(
    core_ref, stride_hbm, counts_hbm, source_hbm, target_ref, field_hbm, nu_hbm,
    out_ref, targets_ref, stride_ref, counts_ref, source_ref, field, nu, sems,
):
    cells = nu.shape[1]
    pad = field.shape[0] - cells
    loads = [
        pltpu.make_async_copy(stride_hbm, stride_ref, sems.at[2]),
        pltpu.make_async_copy(counts_hbm, counts_ref, sems.at[3]),
        pltpu.make_async_copy(source_hbm, source_ref, sems.at[4]),
        pltpu.make_async_copy(field_hbm, field.at[pl.ds(pad, cells)], sems.at[0]),
        pltpu.make_async_copy(nu_hbm, nu, sems.at[1]),
    ]
    for load in loads:
        load.start()
    field[0:pad, :] = jnp.zeros((pad, field.shape[1]), F32)
    width = target_ref.shape[1]
    for sender in range(target_ref.shape[0]):
        targets_ref[0:1, sender * width : (sender + 1) * width] = target_ref[sender : sender + 1, :]
    for load in loads:
        load.wait()
    stride = stride_ref[0]
    slots = source_ref.shape[2]

    @pl.loop(0, source_ref.shape[1])
    def _(grid_row):
        live = counts_ref[0, grid_row]
        for slot in range(slots):
            cell = source_ref[0, grid_row, slot]
            here = field[pl.ds(pad + cell, 1), :]
            radial = here - field[pl.ds(pad + cell - stride, 1), :]
            tangent = here - field[pl.ds(pad - 1 + cell, 1), :]
            swept = nu[0, pl.ds(cell, 1), :] * radial + nu[1, pl.ds(cell, 1), :] * tangent
            out_ref[grid_row, pl.ds(slot, 1), :] = jnp.where(slot < live, swept, 0.0)


def pick(core, sub_field, reluctivity, stride, counts, source_cell, target_row):
    cells, rotor = sub_field.shape
    _, grid_rows, slots = source_cell.shape
    pad = 512
    return pl.pallas_call(
        pick_kernel,
        out_shape=[
            jax.ShapeDtypeStruct((grid_rows, slots, rotor), F32),
            jax.ShapeDtypeStruct((1, target_row.size), jnp.int32),
        ],
        in_specs=[SMEM, HBM, HBM, HBM, VMEM, HBM, HBM],
        out_specs=[VMEM, VMEM],
        scratch_shapes=[
            pltpu.SMEM(stride.shape, jnp.int32),
            pltpu.SMEM(counts.shape, jnp.int32),
            pltpu.SMEM(source_cell.shape, jnp.int32),
            pltpu.VMEM((pad + cells, rotor), F32),
            pltpu.VMEM((2, cells, rotor), F32),
            pltpu.SemaphoreType.DMA((5,)),
        ],
        compiler_params=kernel_params(PICK_LIMIT),
        name="pick",
    )(core, stride, counts, source_cell, target_row, sub_field, reluctivity)


def left_lanes(shape):
    return lax.broadcasted_iota(jnp.int32, shape, 1) < shape[1] // 2


def swap_lanes(value):
    return pltpu.roll(value, value.shape[1] // 2, 1)


def packed(own, other):
    half = own.shape[0] // 2
    return jnp.where(
        left_lanes((half, own.shape[1])),
        own[:half] + swap_lanes(other[:half]),
        swap_lanes(own[half:]) + other[half:],
    )


def three_parts(value):
    high, low = split(value)
    rest = (value - high.astype(F32) - low.astype(F32)).astype(BF16)
    return jnp.concatenate([high, low], axis=1), rest


def interface_rows(block, rows, targets, parts):
    pair, rest = parts
    width = rest.shape[1]
    row = block * rows + lax.broadcasted_iota(jnp.int32, (rows, rest.shape[0]), 0)
    chosen = jnp.where(row == targets, 1.0, 0.0).astype(BF16)
    both = dot(chosen, pair)
    return both[:, :width] + both[:, width:] + dot(chosen, rest)


def fill_interface(block, targets_ref, slots, totals):
    pair, rest = three_parts(slots)

    @pl.loop(0, 2)
    def _(side):
        totals[side] = interface_rows(block, totals.shape[1], targets_ref[side], (pair, rest))


def first_kernel(
    core_ref, own_ref, other_ref, received_ref, swapped_ref, out_ref, slots_ref, targets_ref, totals
):
    targets_ref[0] = own_ref[...]
    targets_ref[1] = other_ref[...]
    received, swapped = received_ref[...], swapped_ref[...]
    left = left_lanes(received.shape)
    low = jnp.where(left, received, swap_lanes(swapped))
    high = jnp.where(left, swap_lanes(received), swapped)
    slots = jnp.where(core_ref[0] == 0, low, high)
    slots_ref[...] = slots
    fill_interface(0, targets_ref, slots, totals)
    out_ref[...] = packed(totals[0], totals[1])


def first_residual(core, own_targets, other_targets, received, swapped, rows):
    rotor = received.shape[1]
    return pl.pallas_call(
        first_kernel,
        out_shape=[
            jax.ShapeDtypeStruct((rows // 2, rotor), F32),
            jax.ShapeDtypeStruct(received.shape, F32),
            jax.ShapeDtypeStruct((2, *own_targets.shape), jnp.int32),
        ],
        in_specs=[SMEM] + [VMEM] * 4,
        out_specs=[VMEM] * 3,
        scratch_shapes=[pltpu.VMEM((2, rows, rotor), F32)],
        compiler_params=kernel_params(),
        name="first",
    )(core, own_targets, other_targets, received, swapped)


def split_sides(load, tiles, first, high_ref, low_ref):
    @pl.loop(0, 2)
    def _(side):
        load(first + side).wait()
        high_ref[side], low_ref[side] = split(tiles[first + side])


def fold_kernel(block, with_diag, *refs):
    earlier = block - 1
    refs = list(refs)
    targets_ref, slots_ref = refs[:2]
    lowers = refs[2:4]
    diags = refs[4:6] if with_diag else []
    at = 4 + len(diags)
    shares = refs[at : at + earlier]
    at += earlier
    started_ref, lower_high, lower_low = refs[at : at + 3]
    at += 3
    diag_outs = refs[at : at + 2] if with_diag else []
    at += len(diag_outs)
    totals, tiles, held, sems, share_sems = refs[at : at + 5]
    base = block * (block - 1) // 2

    for j in range(block):
        for side in range(2):
            at_tile = 2 * j + side
            pltpu.make_async_copy(
                lowers[side].at[base + j], tiles.at[at_tile], sems.at[at_tile]
            ).start()
    for j in range(earlier):
        pltpu.make_async_copy(shares[j], held.at[j], share_sems.at[j]).start()

    def loaded(at_tile):
        return pltpu.make_async_copy(lowers[0].at[0], tiles.at[at_tile], sems.at[at_tile])

    if with_diag:
        diag_tiles, diag_sems = refs[-2:]

        def diag_loaded(side):
            return pltpu.make_async_copy(diags[0].at[0], diag_tiles.at[side], diag_sems.at[side])

        for side in range(2):
            pltpu.make_async_copy(
                diags[side].at[earlier], diag_tiles.at[side], diag_sems.at[side]
            ).start()

    fill_interface(block, targets_ref, slots_ref[...], totals)
    for j in range(earlier):
        pltpu.make_async_copy(shares[j], held.at[j], share_sems.at[j]).wait()
    if earlier:

        @pl.loop(0, 2 * earlier)
        def _(at_tile):
            loaded(at_tile).wait()
            high, low = split(tiles[at_tile])
            side = lax.rem(at_tile, 2)
            totals[side] = totals[side] - split_product(high, low, held[lax.div(at_tile, 2)])

    started_ref[...] = packed(totals[0], totals[1])
    split_sides(loaded, tiles, 2 * earlier, lower_high, lower_low)
    if with_diag:
        split_sides(diag_loaded, diag_tiles, 0, *diag_outs)


def fold(block, targets, slots, lowers, diags, shares):
    _, rows, columns = lowers[0].shape
    rotor = slots.shape[1]
    shapes = [jax.ShapeDtypeStruct((rows // 2, rotor), F32)]
    shapes += [jax.ShapeDtypeStruct((2, rows, columns), BF16)] * 2
    scratch = [
        pltpu.VMEM((2, rows, rotor), F32),
        pltpu.VMEM((2 * block, rows, columns), F32),
        pltpu.VMEM((max(block - 1, 1), columns, rotor), F32),
        pltpu.SemaphoreType.DMA((2 * block,)),
        pltpu.SemaphoreType.DMA((block,)),
    ]
    if diags:
        _, out_rows, depth = diags[0].shape
        shapes += [jax.ShapeDtypeStruct((2, out_rows, depth), BF16)] * 2
        scratch += [pltpu.VMEM((2, out_rows, depth), F32), pltpu.SemaphoreType.DMA((2,))]
    return pl.pallas_call(
        functools.partial(fold_kernel, block, bool(diags)),
        out_shape=shapes,
        in_specs=[VMEM] * 2 + [HBM] * (2 + len(diags)) + [VMEM] * len(shares),
        out_specs=[VMEM] * len(shapes),
        scratch_shapes=scratch,
        compiler_params=kernel_params(WIDE_LIMIT),
        cost_estimate=pl.CostEstimate(
            flops=12 * block * rows * columns * rotor,
            bytes_accessed=8 * (block + 1) * rows * columns,
            transcendentals=0,
        ),
        name="fold",
    )(targets, slots, *lowers, *diags, *shares)


def prepare_kernel(block, own_hbm, other_hbm, high_ref, low_ref, diags, sems):
    for side, hbm in enumerate((own_hbm, other_hbm)):
        pltpu.make_async_copy(hbm.at[block], diags.at[side], sems.at[side]).start()

    def loaded(side):
        return pltpu.make_async_copy(own_hbm.at[block], diags.at[side], sems.at[side])

    split_sides(loaded, diags, 0, high_ref, low_ref)


def prepare(block, diags):
    _, out_rows, depth = diags[0].shape
    return pl.pallas_call(
        functools.partial(prepare_kernel, block),
        out_shape=[jax.ShapeDtypeStruct((2, out_rows, depth), BF16)] * 2,
        in_specs=[HBM] * 2,
        out_specs=[VMEM] * 2,
        scratch_shapes=[
            pltpu.VMEM((2, out_rows, depth), F32),
            pltpu.SemaphoreType.DMA((2,)),
        ],
        compiler_params=kernel_params(WIDE_LIMIT),
        cost_estimate=pl.CostEstimate(
            flops=8 * out_rows * depth,
            bytes_accessed=16 * out_rows * depth,
            transcendentals=0,
        ),
        name="prepare",
    )(*diags)


def lower_kernel(share_ref, high_ref, low_ref, started_ref, out_ref):
    share = share_ref[...]
    out_ref[...] = started_ref[...] - packed(
        split_product(high_ref[0], low_ref[0], share), split_product(high_ref[1], low_ref[1], share)
    )


def lower_product(share, tiles, started):
    return pl.pallas_call(
        lower_kernel,
        out_shape=jax.ShapeDtypeStruct(started.shape, F32),
        in_specs=[VMEM] * 4,
        out_specs=VMEM,
        compiler_params=kernel_params(),
        name="lower",
    )(share, *tiles, started)


def diag_kernel(*refs):
    *residual_refs, high_ref, low_ref, out_ref = refs
    residual = residual_refs[0][...]
    for ref in residual_refs[1:]:
        residual = residual + ref[...]
    turned = swap_lanes(residual)
    left = left_lanes(residual.shape)
    on_left = jnp.concatenate(
        [jnp.where(left, residual, 0.0), jnp.where(left, turned, 0.0)], axis=0
    )
    on_right = jnp.concatenate(
        [jnp.where(left, 0.0, turned), jnp.where(left, 0.0, residual)], axis=0
    )
    out_ref[...] = split_product(high_ref[0], low_ref[0], on_left) + split_product(
        high_ref[1], low_ref[1], on_right
    )


def diag_product(residuals, tiles):
    return pl.pallas_call(
        diag_kernel,
        out_shape=jax.ShapeDtypeStruct((tiles[0].shape[1], residuals[0].shape[1]), F32),
        in_specs=[VMEM] * (len(residuals) + 2),
        out_specs=VMEM,
        compiler_params=kernel_params(),
        name="diag",
    )(*residuals, *tiles)


def piece_kernel(parts_ref, piece_ref, copies_ref):
    piece = jnp.sum(parts_ref[...], axis=0)
    piece_ref[...] = piece
    for peer in range(copies_ref.shape[0]):
        copies_ref[peer] = piece


def piece_and_copies(parts):
    return pl.pallas_call(
        piece_kernel,
        out_shape=[
            jax.ShapeDtypeStruct(parts.shape[1:], F32),
            jax.ShapeDtypeStruct(parts.shape, F32),
        ],
        in_specs=[VMEM],
        out_specs=[VMEM, VMEM],
        compiler_params=kernel_params(),
        name="piece",
    )(parts)


def join_kernel(*refs):
    *piece_refs, out_ref = refs
    for block, piece_ref in enumerate(piece_refs):
        out_ref[block] = piece_ref[...]


def joined(pieces):
    return pl.pallas_call(
        join_kernel,
        out_shape=jax.ShapeDtypeStruct((len(pieces), *pieces[0].shape), F32),
        in_specs=[VMEM] * len(pieces),
        out_specs=VMEM,
        compiler_params=kernel_params(),
        name="join",
    )(*pieces)


def stacked_kernel(core_ref, early_ref, early_other_ref, last_ref, last_other_ref, out_ref):
    left = left_lanes(last_ref.shape)
    first_core = core_ref[0] == 0
    early = early_ref.shape[0]
    for block in range(early + 1):
        own = early_ref[block] if block < early else last_ref[...]
        other = early_other_ref[block] if block < early else last_other_ref[...]
        rows = jnp.where(left, own, other)
        out_ref[block] = jnp.where(first_core, rows, swap_lanes(rows))


def stacked(core, early, early_other, last, last_other):
    return pl.pallas_call(
        stacked_kernel,
        out_shape=jax.ShapeDtypeStruct((early.shape[0] + 1, *last.shape), F32),
        in_specs=[SMEM] + [VMEM] * 4,
        out_specs=VMEM,
        compiler_params=kernel_params(),
        name="stacked",
    )(core, early, early_other, last, last_other)


def other_core(value):
    peers = lax.axis_size("col")
    return lax.ppermute(value, "col", [(i, i ^ 1) for i in range(peers)])


def along_x(value):
    peers = lax.axis_size("col")
    return [value] + [
        lax.ppermute(value, "col", [(i, i ^ apart) for i in range(peers)])
        for apart in (2, 6, 4)
    ]


def per_row(value):
    return lax.all_to_all(value, "row", 0, 0, tiled=True)


def per_device(
    sub_field, reluctivity, stride, counts, source_cell, target_row, lower_tiles, diag_inverse
):
    blocks = diag_inverse.shape[0]
    tile_rows = lower_tiles.shape[1]
    rotor = sub_field.shape[1]
    peers = lax.axis_size("row")
    core = (lax.axis_index("col") % 2).astype(jnp.int32).reshape(1)
    other_diag = other_core(diag_inverse)
    picked, targets = pick(
        core, sub_field, reluctivity, stride, counts, source_cell, target_row[0, 0]
    )
    other_targets = other_core(targets)
    received = per_row(picked).reshape(-1, rotor)
    received, other_diag = lax.optimization_barrier((received, other_diag))
    diags = (diag_inverse, other_diag)

    shares = []
    pieces = []
    residual, slots, targets = first_residual(
        core, targets, other_targets, received, other_core(received), tile_rows
    )
    own_lower, slots = lax.optimization_barrier((lower_tiles, slots))
    lowers = (lower_tiles, other_core(own_lower))
    for block in range(blocks):
        later = block + 1
        if later == blocks:
            residual, pieces = lax.optimization_barrier((residual, pieces))
        residuals = along_x(residual)
        if later < blocks:
            started, lower_high, lower_low, *diag_tiles = fold(
                later, targets, slots, lowers, diags if block else (), shares
            )
        if block == 0 or later == blocks:
            diag_tiles = prepare(block, diags)
        if later == blocks:
            early = joined(pieces)
            diag_tiles, early, early_other = lax.optimization_barrier(
                (diag_tiles, early, other_core(early))
            )
        parts = per_row(diag_product(residuals, diag_tiles).reshape(peers, -1, rotor))
        if later < blocks:
            piece, copies = piece_and_copies(parts)
            pieces.append(piece)
            share = per_row(copies).reshape(-1, rotor)
            shares.append(share)
            residual = lower_product(share, (lower_high, lower_low), started)
    last = jnp.sum(parts, axis=0)
    return stacked(core, early, early_other, last, other_core(last))[:, None]


def solution(mesh):
    placed = (
        P(("row", "col"), None),
        P(None, ("row", "col"), None),
        P(("row", "col")),
        P(("row", "col"), None),
        P(("row", "col"), None, None),
        P("row", "col", None, None),
        P(None, "row", "col"),
        P(None, "col", "row"),
    )
    return jax.shard_map(
        per_device,
        mesh=mesh,
        in_specs=placed,
        out_specs=P(None, "col", "row", None),
        check_vma=False,
    )
```

```python
import functools

import jax
import jax.numpy as jnp
from jax import lax
from jax.experimental import pallas as pl
from jax.experimental.pallas import tpu as pltpu
from jax.sharding import PartitionSpec as P

F32 = jnp.float32
BF16 = jnp.bfloat16
VMEM_LIMIT = 32 * 1024 * 1024
WIDE_LIMIT = 50 * 1024 * 1024
PICK_LIMIT = 54 * 1024 * 1024
VMEM = pl.BlockSpec(memory_space=pltpu.VMEM)
SMEM = pl.BlockSpec(memory_space=pltpu.SMEM)
HBM = pl.BlockSpec(memory_space=pltpu.HBM)


def kernel_params(limit=VMEM_LIMIT):
    return pltpu.CompilerParams(vmem_limit_bytes=limit)


def dot(left, right):
    return jnp.dot(left, right, preferred_element_type=F32)


def split(value):
    high = value.astype(BF16)
    return high, (value - high.astype(F32)).astype(BF16)


def split_product(left_high, left_low, right):
    width = right.shape[1]
    high, low = split(right)
    both = dot(left_high, jnp.concatenate([high, low], axis=1))
    return both[:, :width] + both[:, width:] + dot(left_low, high)


def pick_kernel(
    core_ref, stride_hbm, counts_hbm, source_hbm, target_ref, field_hbm, nu_hbm,
    out_ref, targets_ref, stride_ref, counts_ref, source_ref, field, nu, sems,
):
    cells = nu.shape[1]
    pad = field.shape[0] - cells
    indices = [
        pltpu.make_async_copy(stride_hbm, stride_ref, sems.at[0]),
        pltpu.make_async_copy(counts_hbm, counts_ref, sems.at[1]),
        pltpu.make_async_copy(source_hbm, source_ref, sems.at[2]),
    ]
    parts = 4
    part = cells // parts
    loads = []
    for at in range(parts):
        rows = pl.ds(at * part, part)
        loads.append(
            [
                pltpu.make_async_copy(
                    field_hbm.at[rows], field.at[pl.ds(pad + at * part, part)], sems.at[3 + 3 * at]
                )
            ]
            + [
                pltpu.make_async_copy(
                    nu_hbm.at[side, rows], nu.at[side, rows], sems.at[4 + 3 * at + side]
                )
                for side in range(2)
            ]
        )
    for load in indices + sum(loads, []):
        load.start()
    field[0:pad, :] = jnp.zeros((pad, field.shape[1]), F32)
    width = target_ref.shape[1]
    for sender in range(target_ref.shape[0]):
        targets_ref[0:1, sender * width : (sender + 1) * width] = target_ref[sender : sender + 1, :]
    for load in indices:
        load.wait()
    stride = stride_ref[0]
    slots = source_ref.shape[2]
    chunk = 64
    for at_part in range(parts):
        for load in loads[at_part]:
            load.wait()

        @pl.loop(0, part // chunk)
        def _(step):
            at = pl.multiple_of(at_part * part + step * chunk, chunk)
            here = field[pl.ds(pad + at, chunk), :]
            radial = here - field[pl.ds(pad + at - stride, chunk), :]
            tangent = here - field[pl.ds(pad - 1 + at, chunk), :]
            rows = pl.ds(at, chunk)
            nu[0, rows, :] = nu[0, rows, :] * radial + nu[1, rows, :] * tangent

    @pl.loop(0, source_ref.shape[1])
    def _(grid_row):
        live = counts_ref[0, grid_row]
        for slot in range(slots):
            swept = nu[0, pl.ds(source_ref[0, grid_row, slot], 1), :]
            out_ref[grid_row, pl.ds(slot, 1), :] = jnp.where(slot < live, swept, 0.0)


def pick(core, sub_field, reluctivity, stride, counts, source_cell, target_row):
    cells, rotor = sub_field.shape
    _, grid_rows, slots = source_cell.shape
    pad = 512
    return pl.pallas_call(
        pick_kernel,
        out_shape=[
            jax.ShapeDtypeStruct((grid_rows, slots, rotor), F32),
            jax.ShapeDtypeStruct((1, target_row.size), jnp.int32),
        ],
        in_specs=[SMEM, HBM, HBM, HBM, VMEM, HBM, HBM],
        out_specs=[VMEM, VMEM],
        scratch_shapes=[
            pltpu.SMEM(stride.shape, jnp.int32),
            pltpu.SMEM(counts.shape, jnp.int32),
            pltpu.SMEM(source_cell.shape, jnp.int32),
            pltpu.VMEM((pad + cells, rotor), F32),
            pltpu.VMEM((2, cells, rotor), F32),
            pltpu.SemaphoreType.DMA((15,)),
        ],
        compiler_params=kernel_params(PICK_LIMIT),
        name="pick",
    )(core, stride, counts, source_cell, target_row, sub_field, reluctivity)


def left_lanes(shape):
    return lax.broadcasted_iota(jnp.int32, shape, 1) < shape[1] // 2


def swap_lanes(value):
    return pltpu.roll(value, value.shape[1] // 2, 1)


def packed(own, other):
    half = own.shape[0] // 2
    return jnp.where(
        left_lanes((half, own.shape[1])),
        own[:half] + swap_lanes(other[:half]),
        swap_lanes(own[half:]) + other[half:],
    )


def three_parts(value):
    high, low = split(value)
    rest = (value - high.astype(F32) - low.astype(F32)).astype(BF16)
    return jnp.concatenate([high, low], axis=1), rest


def both_sides(pair):
    return pair.reshape(pair.shape[0] * pair.shape[1], pair.shape[2])


def fill_interface(block, targets_ref, slots, totals):
    pair, rest = three_parts(slots)
    _, rows, width = totals.shape
    row = block * rows + lax.broadcasted_iota(jnp.int32, (rows, slots.shape[0]), 0)
    chosen = jnp.concatenate(
        [jnp.where(row == targets_ref[side], 1.0, 0.0) for side in range(2)], axis=0
    ).astype(BF16)
    both = dot(chosen, pair)
    total = both[:, :width] + both[:, width:] + dot(chosen, rest)
    totals[...] = total.reshape(totals.shape)


def first_kernel(
    core_ref, own_ref, other_ref, received_ref, swapped_ref, out_ref, slots_ref, targets_ref, totals
):
    targets_ref[0] = own_ref[...]
    targets_ref[1] = other_ref[...]
    received, swapped = received_ref[...], swapped_ref[...]
    left = left_lanes(received.shape)
    low = jnp.where(left, received, swap_lanes(swapped))
    high = jnp.where(left, swap_lanes(received), swapped)
    slots = jnp.where(core_ref[0] == 0, low, high)
    slots_ref[...] = slots
    fill_interface(0, targets_ref, slots, totals)
    out_ref[...] = packed(totals[0], totals[1])


def first_residual(core, own_targets, other_targets, received, swapped, rows):
    rotor = received.shape[1]
    return pl.pallas_call(
        first_kernel,
        out_shape=[
            jax.ShapeDtypeStruct((rows // 2, rotor), F32),
            jax.ShapeDtypeStruct(received.shape, F32),
            jax.ShapeDtypeStruct((2, *own_targets.shape), jnp.int32),
        ],
        in_specs=[SMEM] + [VMEM] * 4,
        out_specs=[VMEM] * 3,
        scratch_shapes=[pltpu.VMEM((2, rows, rotor), F32)],
        compiler_params=kernel_params(),
        name="first",
    )(core, own_targets, other_targets, received, swapped)


def split_sides(load, tiles, first, high_ref, low_ref):
    @pl.loop(0, 2)
    def _(side):
        load(first + side).wait()
        high_ref[side], low_ref[side] = split(tiles[first + side])


def fold_kernel(block, with_diag, *refs):
    earlier = block - 1
    refs = list(refs)
    targets_ref, slots_ref = refs[:2]
    lowers = refs[2:4]
    diags = refs[4:6] if with_diag else []
    at = 4 + len(diags)
    shares = refs[at : at + earlier]
    at += earlier
    started_ref, lower_high, lower_low = refs[at : at + 3]
    at += 3
    diag_outs = refs[at : at + 2] if with_diag else []
    at += len(diag_outs)
    totals, tiles, held, sems, share_sems = refs[at : at + 5]
    base = block * (block - 1) // 2

    for j in range(block):
        for side in range(2):
            at_tile = 2 * j + side
            pltpu.make_async_copy(
                lowers[side].at[base + j], tiles.at[at_tile], sems.at[at_tile]
            ).start()
    for j in range(earlier):
        pltpu.make_async_copy(shares[j], held.at[j], share_sems.at[j]).start()

    def loaded(at_tile):
        return pltpu.make_async_copy(lowers[0].at[0], tiles.at[at_tile], sems.at[at_tile])

    if with_diag:
        diag_tiles, diag_sems = refs[-2:]

        def diag_loaded(side):
            return pltpu.make_async_copy(diags[0].at[0], diag_tiles.at[side], diag_sems.at[side])

        for side in range(2):
            pltpu.make_async_copy(
                diags[side].at[earlier], diag_tiles.at[side], diag_sems.at[side]
            ).start()

    fill_interface(block, targets_ref, slots_ref[...], totals)
    for j in range(earlier):
        pltpu.make_async_copy(shares[j], held.at[j], share_sems.at[j]).wait()
    if earlier:

        @pl.loop(0, earlier)
        def _(j):
            loaded(2 * j).wait()
            loaded(2 * j + 1).wait()
            high, low = split(both_sides(tiles[pl.ds(2 * j, 2)]))
            totals[...] = totals[...] - split_product(high, low, held[j]).reshape(totals.shape)

    started_ref[...] = packed(totals[0], totals[1])
    split_sides(loaded, tiles, 2 * earlier, lower_high, lower_low)
    if with_diag:
        split_sides(diag_loaded, diag_tiles, 0, *diag_outs)


def fold(block, targets, slots, lowers, diags, shares):
    _, rows, columns = lowers[0].shape
    rotor = slots.shape[1]
    shapes = [jax.ShapeDtypeStruct((rows // 2, rotor), F32)]
    shapes += [jax.ShapeDtypeStruct((2, rows, columns), BF16)] * 2
    scratch = [
        pltpu.VMEM((2, rows, rotor), F32),
        pltpu.VMEM((2 * block, rows, columns), F32),
        pltpu.VMEM((max(block - 1, 1), columns, rotor), F32),
        pltpu.SemaphoreType.DMA((2 * block,)),
        pltpu.SemaphoreType.DMA((block,)),
    ]
    if diags:
        _, out_rows, depth = diags[0].shape
        shapes += [jax.ShapeDtypeStruct((2, out_rows, depth), BF16)] * 2
        scratch += [pltpu.VMEM((2, out_rows, depth), F32), pltpu.SemaphoreType.DMA((2,))]
    return pl.pallas_call(
        functools.partial(fold_kernel, block, bool(diags)),
        out_shape=shapes,
        in_specs=[VMEM] * 2 + [HBM] * (2 + len(diags)) + [VMEM] * len(shares),
        out_specs=[VMEM] * len(shapes),
        scratch_shapes=scratch,
        compiler_params=kernel_params(WIDE_LIMIT),
        cost_estimate=pl.CostEstimate(
            flops=12 * block * rows * columns * rotor,
            bytes_accessed=8 * (block + 1) * rows * columns,
            transcendentals=0,
        ),
        name="fold",
    )(targets, slots, *lowers, *diags, *shares)


def prepare_kernel(block, own_hbm, other_hbm, high_ref, low_ref, diags, sems):
    for side, hbm in enumerate((own_hbm, other_hbm)):
        pltpu.make_async_copy(hbm.at[block], diags.at[side], sems.at[side]).start()

    def loaded(side):
        return pltpu.make_async_copy(own_hbm.at[block], diags.at[side], sems.at[side])

    split_sides(loaded, diags, 0, high_ref, low_ref)


def prepare(block, diags):
    _, out_rows, depth = diags[0].shape
    return pl.pallas_call(
        functools.partial(prepare_kernel, block),
        out_shape=[jax.ShapeDtypeStruct((2, out_rows, depth), BF16)] * 2,
        in_specs=[HBM] * 2,
        out_specs=[VMEM] * 2,
        scratch_shapes=[
            pltpu.VMEM((2, out_rows, depth), F32),
            pltpu.SemaphoreType.DMA((2,)),
        ],
        compiler_params=kernel_params(WIDE_LIMIT),
        cost_estimate=pl.CostEstimate(
            flops=8 * out_rows * depth,
            bytes_accessed=16 * out_rows * depth,
            transcendentals=0,
        ),
        name="prepare",
    )(*diags)


def lower_kernel(share_ref, high_ref, low_ref, started_ref, out_ref):
    value = split_product(both_sides(high_ref[...]), both_sides(low_ref[...]), share_ref[...])
    rows = high_ref.shape[1]
    out_ref[...] = started_ref[...] - packed(value[:rows], value[rows:])


def lower_product(share, tiles, started):
    return pl.pallas_call(
        lower_kernel,
        out_shape=jax.ShapeDtypeStruct(started.shape, F32),
        in_specs=[VMEM] * 4,
        out_specs=VMEM,
        compiler_params=kernel_params(),
        name="lower",
    )(share, *tiles, started)


def diag_kernel(*refs):
    *residual_refs, high_ref, low_ref, out_ref = refs
    residual = residual_refs[0][...]
    for ref in residual_refs[1:]:
        residual = residual + ref[...]
    turned = swap_lanes(residual)
    left = left_lanes(residual.shape)
    on_left = jnp.concatenate(
        [jnp.where(left, residual, 0.0), jnp.where(left, turned, 0.0)], axis=0
    )
    on_right = jnp.concatenate(
        [jnp.where(left, 0.0, turned), jnp.where(left, 0.0, residual)], axis=0
    )
    out_ref[...] = split_product(high_ref[0], low_ref[0], on_left) + split_product(
        high_ref[1], low_ref[1], on_right
    )


def diag_product(residuals, tiles):
    return pl.pallas_call(
        diag_kernel,
        out_shape=jax.ShapeDtypeStruct((tiles[0].shape[1], residuals[0].shape[1]), F32),
        in_specs=[VMEM] * (len(residuals) + 2),
        out_specs=VMEM,
        compiler_params=kernel_params(),
        name="diag",
    )(*residuals, *tiles)


def piece_kernel(parts_ref, piece_ref, copies_ref):
    piece = jnp.sum(parts_ref[...], axis=0)
    piece_ref[...] = piece
    for peer in range(copies_ref.shape[0]):
        copies_ref[peer] = piece


def piece_and_copies(parts):
    return pl.pallas_call(
        piece_kernel,
        out_shape=[
            jax.ShapeDtypeStruct(parts.shape[1:], F32),
            jax.ShapeDtypeStruct(parts.shape, F32),
        ],
        in_specs=[VMEM],
        out_specs=[VMEM, VMEM],
        compiler_params=kernel_params(),
        name="piece",
    )(parts)


def join_kernel(*refs):
    *piece_refs, out_ref = refs
    for block, piece_ref in enumerate(piece_refs):
        out_ref[block] = piece_ref[...]


def joined(pieces):
    return pl.pallas_call(
        join_kernel,
        out_shape=jax.ShapeDtypeStruct((len(pieces), *pieces[0].shape), F32),
        in_specs=[VMEM] * len(pieces),
        out_specs=VMEM,
        compiler_params=kernel_params(),
        name="join",
    )(*pieces)


def stacked_kernel(core_ref, early_ref, early_other_ref, last_ref, last_other_ref, out_ref):
    left = left_lanes(last_ref.shape)
    first_core = core_ref[0] == 0
    early = early_ref.shape[0]
    for block in range(early + 1):
        own = early_ref[block] if block < early else last_ref[...]
        other = early_other_ref[block] if block < early else last_other_ref[...]
        rows = jnp.where(left, own, other)
        out_ref[block] = jnp.where(first_core, rows, swap_lanes(rows))


def stacked(core, early, early_other, last, last_other):
    return pl.pallas_call(
        stacked_kernel,
        out_shape=jax.ShapeDtypeStruct((early.shape[0] + 1, *last.shape), F32),
        in_specs=[SMEM] + [VMEM] * 4,
        out_specs=VMEM,
        compiler_params=kernel_params(),
        name="stacked",
    )(core, early, early_other, last, last_other)


def other_core(value):
    peers = lax.axis_size("col")
    return lax.ppermute(value, "col", [(i, i ^ 1) for i in range(peers)])


def along_x(value):
    peers = lax.axis_size("col")
    return [value] + [
        lax.ppermute(value, "col", [(i, i ^ apart) for i in range(peers)])
        for apart in (2, 6, 4)
    ]


def per_row(value):
    return lax.all_to_all(value, "row", 0, 0, tiled=True)


def per_device(
    sub_field, reluctivity, stride, counts, source_cell, target_row, lower_tiles, diag_inverse
):
    blocks = diag_inverse.shape[0]
    tile_rows = lower_tiles.shape[1]
    rotor = sub_field.shape[1]
    peers = lax.axis_size("row")
    core = (lax.axis_index("col") % 2).astype(jnp.int32).reshape(1)
    other_diag = other_core(diag_inverse)
    picked, targets = pick(
        core, sub_field, reluctivity, stride, counts, source_cell, target_row[0, 0]
    )
    other_targets = other_core(targets)
    received = per_row(picked).reshape(-1, rotor)
    received, other_diag = lax.optimization_barrier((received, other_diag))
    diags = (diag_inverse, other_diag)

    shares = []
    pieces = []
    residual, slots, targets = first_residual(
        core, targets, other_targets, received, other_core(received), tile_rows
    )
    own_lower, slots = lax.optimization_barrier((lower_tiles, slots))
    lowers = (lower_tiles, other_core(own_lower))
    for block in range(blocks):
        later = block + 1
        if later == blocks:
            residual, pieces = lax.optimization_barrier((residual, pieces))
        residuals = along_x(residual)
        if later < blocks:
            started, lower_high, lower_low, *diag_tiles = fold(
                later, targets, slots, lowers, diags if block else (), shares
            )
        if block == 0 or later == blocks:
            diag_tiles = prepare(block, diags)
        if later == blocks:
            early = joined(pieces)
            diag_tiles, early, early_other = lax.optimization_barrier(
                (diag_tiles, early, other_core(early))
            )
        parts = per_row(diag_product(residuals, diag_tiles).reshape(peers, -1, rotor))
        if later < blocks:
            piece, copies = piece_and_copies(parts)
            pieces.append(piece)
            share = per_row(copies).reshape(-1, rotor)
            shares.append(share)
            residual = lower_product(share, (lower_high, lower_low), started)
    last = jnp.sum(parts, axis=0)
    return stacked(core, early, early_other, last, other_core(last))[:, None]


def solution(mesh):
    placed = (
        P(("row", "col"), None),
        P(None, ("row", "col"), None),
        P(("row", "col")),
        P(("row", "col"), None),
        P(("row", "col"), None, None),
        P("row", "col", None, None),
        P(None, "row", "col"),
        P(None, "col", "row"),
    )
    return jax.shard_map(
        per_device,
        mesh=mesh,
        in_specs=placed,
        out_specs=P(None, "col", "row", None),
        check_vma=False,
    )
```

```python
import functools

import jax
import jax.numpy as jnp
from jax import lax
from jax.experimental import pallas as pl
from jax.experimental.pallas import tpu as pltpu
from jax.sharding import PartitionSpec as P

F32 = jnp.float32
BF16 = jnp.bfloat16
VMEM_LIMIT = 32 * 1024 * 1024
WIDE_LIMIT = 50 * 1024 * 1024
PICK_LIMIT = 54 * 1024 * 1024
VMEM = pl.BlockSpec(memory_space=pltpu.VMEM)
SMEM = pl.BlockSpec(memory_space=pltpu.SMEM)
HBM = pl.BlockSpec(memory_space=pltpu.HBM)


def kernel_params(limit=VMEM_LIMIT):
    return pltpu.CompilerParams(vmem_limit_bytes=limit)


def dot(left, right):
    return jnp.dot(left, right, preferred_element_type=F32)


def split(value):
    high = value.astype(BF16)
    return high, (value - high.astype(F32)).astype(BF16)


def split_product(left_high, left_low, right):
    width = right.shape[1]
    high, low = split(right)
    both = dot(left_high, jnp.concatenate([high, low], axis=1))
    return both[:, :width] + both[:, width:] + dot(left_low, high)


def pick_kernel(
    core_ref, stride_hbm, counts_hbm, source_hbm, target_ref, field_hbm, nu_hbm,
    out_ref, targets_ref, stride_ref, counts_ref, source_ref, field, nu, sems,
):
    cells = nu.shape[1]
    pad = field.shape[0] - cells
    indices = [
        pltpu.make_async_copy(stride_hbm, stride_ref, sems.at[0]),
        pltpu.make_async_copy(counts_hbm, counts_ref, sems.at[1]),
        pltpu.make_async_copy(source_hbm, source_ref, sems.at[2]),
    ]
    parts = 4
    part = cells // parts
    loads = []
    for at in range(parts):
        rows = pl.ds(at * part, part)
        loads.append(
            [
                pltpu.make_async_copy(
                    field_hbm.at[rows], field.at[pl.ds(pad + at * part, part)], sems.at[3 + 3 * at]
                )
            ]
            + [
                pltpu.make_async_copy(
                    nu_hbm.at[side, rows], nu.at[side, rows], sems.at[4 + 3 * at + side]
                )
                for side in range(2)
            ]
        )
    for load in indices + sum(loads, []):
        load.start()
    field[0:pad, :] = jnp.zeros((pad, field.shape[1]), F32)
    width = target_ref.shape[1]
    for sender in range(target_ref.shape[0]):
        targets_ref[0:1, sender * width : (sender + 1) * width] = target_ref[sender : sender + 1, :]
    for load in indices:
        load.wait()
    stride = stride_ref[0]
    slots = source_ref.shape[2]
    chunk = 64
    for at_part in range(parts):
        for load in loads[at_part]:
            load.wait()

        @pl.loop(0, part // chunk)
        def _(step):
            at = pl.multiple_of(at_part * part + step * chunk, chunk)
            here = field[pl.ds(pad + at, chunk), :]
            radial = here - field[pl.ds(pad + at - stride, chunk), :]
            tangent = here - field[pl.ds(pad - 1 + at, chunk), :]
            rows = pl.ds(at, chunk)
            nu[0, rows, :] = nu[0, rows, :] * radial + nu[1, rows, :] * tangent

    @pl.loop(0, source_ref.shape[1])
    def _(grid_row):
        live = counts_ref[0, grid_row]
        for slot in range(slots):
            swept = nu[0, pl.ds(source_ref[0, grid_row, slot], 1), :]
            out_ref[grid_row, pl.ds(slot, 1), :] = jnp.where(slot < live, swept, 0.0)


def pick(core, sub_field, reluctivity, stride, counts, source_cell, target_row):
    cells, rotor = sub_field.shape
    _, grid_rows, slots = source_cell.shape
    pad = 512
    return pl.pallas_call(
        pick_kernel,
        out_shape=[
            jax.ShapeDtypeStruct((grid_rows, slots, rotor), F32),
            jax.ShapeDtypeStruct((1, target_row.size), jnp.int32),
        ],
        in_specs=[SMEM, HBM, HBM, HBM, VMEM, HBM, HBM],
        out_specs=[VMEM, VMEM],
        scratch_shapes=[
            pltpu.SMEM(stride.shape, jnp.int32),
            pltpu.SMEM(counts.shape, jnp.int32),
            pltpu.SMEM(source_cell.shape, jnp.int32),
            pltpu.VMEM((pad + cells, rotor), F32),
            pltpu.VMEM((2, cells, rotor), F32),
            pltpu.SemaphoreType.DMA((15,)),
        ],
        compiler_params=kernel_params(PICK_LIMIT),
        name="pick",
    )(core, stride, counts, source_cell, target_row, sub_field, reluctivity)


def left_lanes(shape):
    return lax.broadcasted_iota(jnp.int32, shape, 1) < shape[1] // 2


def swap_lanes(value):
    return pltpu.roll(value, value.shape[1] // 2, 1)


def packed(own, other):
    half = own.shape[0] // 2
    return jnp.where(
        left_lanes((half, own.shape[1])),
        own[:half] + swap_lanes(other[:half]),
        swap_lanes(own[half:]) + other[half:],
    )


def three_parts(value):
    high, low = split(value)
    rest = (value - high.astype(F32) - low.astype(F32)).astype(BF16)
    return jnp.concatenate([high, low], axis=1), rest


def both_sides(pair):
    return pair.reshape(pair.shape[0] * pair.shape[1], pair.shape[2])


def fill_interface(block, targets_ref, slots, totals):
    pair, rest = three_parts(slots)
    _, rows, width = totals.shape
    row = block * rows + lax.broadcasted_iota(jnp.int32, (rows, slots.shape[0]), 0)
    chosen = jnp.concatenate(
        [jnp.where(row == targets_ref[side], 1.0, 0.0) for side in range(2)], axis=0
    ).astype(BF16)
    both = dot(chosen, pair)
    total = both[:, :width] + both[:, width:] + dot(chosen, rest)
    totals[...] = total.reshape(totals.shape)


def first_kernel(
    core_ref, own_ref, other_ref, received_ref, swapped_ref, out_ref, slots_ref, targets_ref, totals
):
    targets_ref[0] = own_ref[...]
    targets_ref[1] = other_ref[...]
    received, swapped = received_ref[...], swapped_ref[...]
    left = left_lanes(received.shape)
    low = jnp.where(left, received, swap_lanes(swapped))
    high = jnp.where(left, swap_lanes(received), swapped)
    slots = jnp.where(core_ref[0] == 0, low, high)
    slots_ref[...] = slots
    fill_interface(0, targets_ref, slots, totals)
    out_ref[...] = packed(totals[0], totals[1])


def first_residual(core, own_targets, other_targets, received, swapped, rows):
    rotor = received.shape[1]
    return pl.pallas_call(
        first_kernel,
        out_shape=[
            jax.ShapeDtypeStruct((rows // 2, rotor), F32),
            jax.ShapeDtypeStruct(received.shape, F32),
            jax.ShapeDtypeStruct((2, *own_targets.shape), jnp.int32),
        ],
        in_specs=[SMEM] + [VMEM] * 4,
        out_specs=[VMEM] * 3,
        scratch_shapes=[pltpu.VMEM((2, rows, rotor), F32)],
        compiler_params=kernel_params(),
        name="first",
    )(core, own_targets, other_targets, received, swapped)


def split_sides(load, tiles, first, high_ref, low_ref):
    @pl.loop(0, 2)
    def _(side):
        load(first + side).wait()
        high_ref[side], low_ref[side] = split(tiles[first + side])


def fold_kernel(block, with_diag, skip, ahead, *refs):
    earlier = block - 1
    later, count = ahead
    refs = list(refs)
    targets_ref, slots_ref = refs[:2]
    lowers = refs[2:4]
    diags = refs[4:6] if with_diag else []
    at = 4 + len(diags)
    shares = refs[at : at + earlier]
    at += earlier
    carried = refs[at : at + 1] if skip else []
    at += len(carried)
    started_ref, lower_high, lower_low = refs[at : at + 3]
    at += 3
    diag_outs = refs[at : at + 2] if with_diag else []
    at += len(diag_outs)
    ahead_outs = refs[at : at + 1] if count else []
    at += len(ahead_outs)
    totals, tiles, held, sems, share_sems = refs[at : at + 5]
    base = block * (block - 1) // 2

    wanted = [base + j for j in range(skip, block)]
    wanted += [later * (later - 1) // 2 + j for j in range(count)]
    for index, pair in enumerate(wanted):
        for side in range(2):
            at_tile = 2 * index + side
            pltpu.make_async_copy(
                lowers[side].at[pair], tiles.at[at_tile], sems.at[at_tile]
            ).start()
    for j in range(earlier):
        pltpu.make_async_copy(shares[j], held.at[j], share_sems.at[j]).start()

    def loaded(at_tile):
        return pltpu.make_async_copy(lowers[0].at[0], tiles.at[at_tile], sems.at[at_tile])

    if with_diag:
        diag_tiles, diag_sems = refs[-2:]

        def diag_loaded(side):
            return pltpu.make_async_copy(diags[0].at[0], diag_tiles.at[side], diag_sems.at[side])

        for side in range(2):
            pltpu.make_async_copy(
                diags[side].at[earlier], diag_tiles.at[side], diag_sems.at[side]
            ).start()

    fill_interface(block, targets_ref, slots_ref[...], totals)
    for j in range(earlier):
        pltpu.make_async_copy(shares[j], held.at[j], share_sems.at[j]).wait()
    if skip:
        totals[...] = totals[...] + carried[0][...]

    def subtract(total_ref, at_tile, share):
        loaded(at_tile).wait()
        loaded(at_tile + 1).wait()
        high, low = split(both_sides(tiles[pl.ds(at_tile, 2)]))
        total_ref[...] = total_ref[...] - split_product(high, low, held[share]).reshape(
            total_ref.shape
        )

    if earlier > skip:

        @pl.loop(skip, earlier)
        def _(j):
            subtract(totals, 2 * (j - skip), j)

    started_ref[...] = packed(totals[0], totals[1])
    split_sides(loaded, tiles, 2 * (earlier - skip), lower_high, lower_low)
    if count:
        ahead_outs[0][...] = jnp.zeros(totals.shape, F32)

        @pl.loop(0, count)
        def _(j):
            subtract(ahead_outs[0], 2 * (block - skip + j), j)

    if with_diag:
        split_sides(diag_loaded, diag_tiles, 0, *diag_outs)


def fold(block, targets, slots, lowers, diags, shares, carried=(), skip=0, ahead=(0, 0)):
    n_pairs = block - skip + ahead[1]
    _, rows, columns = lowers[0].shape
    rotor = slots.shape[1]
    shapes = [jax.ShapeDtypeStruct((rows // 2, rotor), F32)]
    shapes += [jax.ShapeDtypeStruct((2, rows, columns), BF16)] * 2
    scratch = [
        pltpu.VMEM((2, rows, rotor), F32),
        pltpu.VMEM((2 * n_pairs, rows, columns), F32),
        pltpu.VMEM((max(block - 1, 1), columns, rotor), F32),
        pltpu.SemaphoreType.DMA((2 * n_pairs,)),
        pltpu.SemaphoreType.DMA((block,)),
    ]
    if diags:
        _, out_rows, depth = diags[0].shape
        shapes += [jax.ShapeDtypeStruct((2, out_rows, depth), BF16)] * 2
        scratch += [pltpu.VMEM((2, out_rows, depth), F32), pltpu.SemaphoreType.DMA((2,))]
    if ahead[1]:
        shapes += [jax.ShapeDtypeStruct((2, rows, rotor), F32)]
    return pl.pallas_call(
        functools.partial(fold_kernel, block, bool(diags), skip, ahead),
        out_shape=shapes,
        in_specs=[VMEM] * 2 + [HBM] * (2 + len(diags)) + [VMEM] * (len(shares) + len(carried)),
        out_specs=[VMEM] * len(shapes),
        scratch_shapes=scratch,
        compiler_params=kernel_params(WIDE_LIMIT),
        cost_estimate=pl.CostEstimate(
            flops=12 * n_pairs * rows * columns * rotor,
            bytes_accessed=8 * (n_pairs + 1) * rows * columns,
            transcendentals=0,
        ),
        name="fold",
    )(targets, slots, *lowers, *diags, *shares, *carried)


def prepare_kernel(block, own_hbm, other_hbm, high_ref, low_ref, diags, sems):
    for side, hbm in enumerate((own_hbm, other_hbm)):
        pltpu.make_async_copy(hbm.at[block], diags.at[side], sems.at[side]).start()

    def loaded(side):
        return pltpu.make_async_copy(own_hbm.at[block], diags.at[side], sems.at[side])

    split_sides(loaded, diags, 0, high_ref, low_ref)


def prepare(block, diags):
    _, out_rows, depth = diags[0].shape
    return pl.pallas_call(
        functools.partial(prepare_kernel, block),
        out_shape=[jax.ShapeDtypeStruct((2, out_rows, depth), BF16)] * 2,
        in_specs=[HBM] * 2,
        out_specs=[VMEM] * 2,
        scratch_shapes=[
            pltpu.VMEM((2, out_rows, depth), F32),
            pltpu.SemaphoreType.DMA((2,)),
        ],
        compiler_params=kernel_params(WIDE_LIMIT),
        cost_estimate=pl.CostEstimate(
            flops=8 * out_rows * depth,
            bytes_accessed=16 * out_rows * depth,
            transcendentals=0,
        ),
        name="prepare",
    )(*diags)


def lower_kernel(share_ref, high_ref, low_ref, started_ref, out_ref):
    value = split_product(both_sides(high_ref[...]), both_sides(low_ref[...]), share_ref[...])
    rows = high_ref.shape[1]
    out_ref[...] = started_ref[...] - packed(value[:rows], value[rows:])


def lower_product(share, tiles, started):
    return pl.pallas_call(
        lower_kernel,
        out_shape=jax.ShapeDtypeStruct(started.shape, F32),
        in_specs=[VMEM] * 4,
        out_specs=VMEM,
        compiler_params=kernel_params(),
        name="lower",
    )(share, *tiles, started)


def diag_kernel(*refs):
    *residual_refs, high_ref, low_ref, out_ref = refs
    residual = residual_refs[0][...]
    for ref in residual_refs[1:]:
        residual = residual + ref[...]
    turned = swap_lanes(residual)
    left = left_lanes(residual.shape)
    on_left = jnp.concatenate(
        [jnp.where(left, residual, 0.0), jnp.where(left, turned, 0.0)], axis=0
    )
    on_right = jnp.concatenate(
        [jnp.where(left, 0.0, turned), jnp.where(left, 0.0, residual)], axis=0
    )
    out_ref[...] = split_product(high_ref[0], low_ref[0], on_left) + split_product(
        high_ref[1], low_ref[1], on_right
    )


def diag_product(residuals, tiles):
    return pl.pallas_call(
        diag_kernel,
        out_shape=jax.ShapeDtypeStruct((tiles[0].shape[1], residuals[0].shape[1]), F32),
        in_specs=[VMEM] * (len(residuals) + 2),
        out_specs=VMEM,
        compiler_params=kernel_params(),
        name="diag",
    )(*residuals, *tiles)


def piece_kernel(parts_ref, piece_ref, copies_ref):
    piece = jnp.sum(parts_ref[...], axis=0)
    piece_ref[...] = piece
    for peer in range(copies_ref.shape[0]):
        copies_ref[peer] = piece


def piece_and_copies(parts):
    return pl.pallas_call(
        piece_kernel,
        out_shape=[
            jax.ShapeDtypeStruct(parts.shape[1:], F32),
            jax.ShapeDtypeStruct(parts.shape, F32),
        ],
        in_specs=[VMEM],
        out_specs=[VMEM, VMEM],
        compiler_params=kernel_params(),
        name="piece",
    )(parts)


def join_kernel(*refs):
    *piece_refs, out_ref = refs
    for block, piece_ref in enumerate(piece_refs):
        out_ref[block] = piece_ref[...]


def joined(pieces):
    return pl.pallas_call(
        join_kernel,
        out_shape=jax.ShapeDtypeStruct((len(pieces), *pieces[0].shape), F32),
        in_specs=[VMEM] * len(pieces),
        out_specs=VMEM,
        compiler_params=kernel_params(),
        name="join",
    )(*pieces)


def stacked_kernel(core_ref, early_ref, early_other_ref, last_ref, last_other_ref, out_ref):
    left = left_lanes(last_ref.shape)
    first_core = core_ref[0] == 0
    early = early_ref.shape[0]
    for block in range(early + 1):
        own = early_ref[block] if block < early else last_ref[...]
        other = early_other_ref[block] if block < early else last_other_ref[...]
        rows = jnp.where(left, own, other)
        out_ref[block] = jnp.where(first_core, rows, swap_lanes(rows))


def stacked(core, early, early_other, last, last_other):
    return pl.pallas_call(
        stacked_kernel,
        out_shape=jax.ShapeDtypeStruct((early.shape[0] + 1, *last.shape), F32),
        in_specs=[SMEM] + [VMEM] * 4,
        out_specs=VMEM,
        compiler_params=kernel_params(),
        name="stacked",
    )(core, early, early_other, last, last_other)


def other_core(value):
    peers = lax.axis_size("col")
    return lax.ppermute(value, "col", [(i, i ^ 1) for i in range(peers)])


def along_x(value):
    peers = lax.axis_size("col")
    return [value] + [
        lax.ppermute(value, "col", [(i, i ^ apart) for i in range(peers)])
        for apart in (2, 6, 4)
    ]


def per_row(value):
    return lax.all_to_all(value, "row", 0, 0, tiled=True)


def per_device(
    sub_field, reluctivity, stride, counts, source_cell, target_row, lower_tiles, diag_inverse
):
    blocks = diag_inverse.shape[0]
    tile_rows = lower_tiles.shape[1]
    rotor = sub_field.shape[1]
    peers = lax.axis_size("row")
    core = (lax.axis_index("col") % 2).astype(jnp.int32).reshape(1)
    other_diag = other_core(diag_inverse)
    picked, targets = pick(
        core, sub_field, reluctivity, stride, counts, source_cell, target_row[0, 0]
    )
    other_targets = other_core(targets)
    received = per_row(picked).reshape(-1, rotor)
    received, other_diag = lax.optimization_barrier((received, other_diag))
    diags = (diag_inverse, other_diag)

    shares = []
    pieces = []
    waiting = {}
    residual, slots, targets = first_residual(
        core, targets, other_targets, received, other_core(received), tile_rows
    )
    own_lower, slots = lax.optimization_barrier((lower_tiles, slots))
    lowers = (lower_tiles, other_core(own_lower))
    for block in range(blocks):
        later = block + 1
        if later == blocks:
            residual, pieces = lax.optimization_barrier((residual, pieces))
        residuals = along_x(residual)
        if later < blocks:
            ahead = {2: (blocks - 2, 1), 3: (blocks - 1, 2)}.get(later, (0, 0))
            carried = waiting.pop(later, None)
            started, lower_high, lower_low, *diag_tiles = fold(
                later,
                targets,
                slots,
                lowers,
                diags if block else (),
                shares,
                () if carried is None else (carried[0],),
                0 if carried is None else carried[1],
                ahead,
            )
            if ahead[1]:
                waiting[ahead[0]] = (diag_tiles.pop(), ahead[1])
        if block == 0 or later == blocks:
            diag_tiles = prepare(block, diags)
        if later == blocks:
            early = joined(pieces)
            diag_tiles, early, early_other = lax.optimization_barrier(
                (diag_tiles, early, other_core(early))
            )
        parts = per_row(diag_product(residuals, diag_tiles).reshape(peers, -1, rotor))
        if later < blocks:
            piece, copies = piece_and_copies(parts)
            pieces.append(piece)
            share = per_row(copies).reshape(-1, rotor)
            shares.append(share)
            residual = lower_product(share, (lower_high, lower_low), started)
    last = jnp.sum(parts, axis=0)
    return stacked(core, early, early_other, last, other_core(last))[:, None]


def solution(mesh):
    placed = (
        P(("row", "col"), None),
        P(None, ("row", "col"), None),
        P(("row", "col")),
        P(("row", "col"), None),
        P(("row", "col"), None, None),
        P("row", "col", None, None),
        P(None, "row", "col"),
        P(None, "col", "row"),
    )
    return jax.shard_map(
        per_device,
        mesh=mesh,
        in_specs=placed,
        out_specs=P(None, "col", "row", None),
        check_vma=False,
    )
```

```python
import functools

import jax
import jax.numpy as jnp
from jax import lax
from jax.experimental import pallas as pl
from jax.experimental.pallas import tpu as pltpu
from jax.sharding import PartitionSpec as P

F32 = jnp.float32
BF16 = jnp.bfloat16
VMEM_LIMIT = 32 * 1024 * 1024
WIDE_LIMIT = 50 * 1024 * 1024
PICK_LIMIT = 54 * 1024 * 1024
VMEM = pl.BlockSpec(memory_space=pltpu.VMEM)
SMEM = pl.BlockSpec(memory_space=pltpu.SMEM)
HBM = pl.BlockSpec(memory_space=pltpu.HBM)


def kernel_params(limit=VMEM_LIMIT):
    return pltpu.CompilerParams(vmem_limit_bytes=limit)


def dot(left, right):
    return jnp.dot(left, right, preferred_element_type=F32)


def split(value):
    high = value.astype(BF16)
    return high, (value - high.astype(F32)).astype(BF16)


def split_product(left_high, left_low, right):
    width = right.shape[1]
    high, low = split(right)
    both = dot(left_high, jnp.concatenate([high, low], axis=1))
    return both[:, :width] + both[:, width:] + dot(left_low, high)


def pick_kernel(
    core_ref, stride_hbm, counts_hbm, source_hbm, target_ref, field_hbm, nu_hbm,
    out_ref, targets_ref, stride_ref, counts_ref, source_ref, field, nu, sems,
):
    cells = nu.shape[1]
    pad = field.shape[0] - cells
    indices = [
        pltpu.make_async_copy(stride_hbm, stride_ref, sems.at[0]),
        pltpu.make_async_copy(counts_hbm, counts_ref, sems.at[1]),
        pltpu.make_async_copy(source_hbm, source_ref, sems.at[2]),
    ]
    parts = 4
    part = cells // parts
    loads = []
    for at in range(parts):
        rows = pl.ds(at * part, part)
        loads.append(
            [
                pltpu.make_async_copy(
                    field_hbm.at[rows], field.at[pl.ds(pad + at * part, part)], sems.at[3 + 3 * at]
                )
            ]
            + [
                pltpu.make_async_copy(
                    nu_hbm.at[side, rows], nu.at[side, rows], sems.at[4 + 3 * at + side]
                )
                for side in range(2)
            ]
        )
    for load in indices + sum(loads, []):
        load.start()
    field[0:pad, :] = jnp.zeros((pad, field.shape[1]), F32)
    width = target_ref.shape[1]
    for sender in range(target_ref.shape[0]):
        targets_ref[0:1, sender * width : (sender + 1) * width] = target_ref[sender : sender + 1, :]
    for load in indices:
        load.wait()
    stride = stride_ref[0]
    slots = source_ref.shape[2]
    chunk = 256
    for at_part in range(parts):
        for load in loads[at_part]:
            load.wait()

        @pl.loop(0, part // chunk)
        def _(step):
            at = pl.multiple_of(at_part * part + step * chunk, chunk)
            here = field[pl.ds(pad + at, chunk), :]
            radial = here - field[pl.ds(pad + at - stride, chunk), :]
            tangent = here - field[pl.ds(pad - 1 + at, chunk), :]
            rows = pl.ds(at, chunk)
            nu[0, rows, :] = nu[0, rows, :] * radial + nu[1, rows, :] * tangent

    @pl.loop(0, source_ref.shape[1])
    def _(grid_row):
        live = counts_ref[0, grid_row]
        for slot in range(slots):
            swept = nu[0, pl.ds(source_ref[0, grid_row, slot], 1), :]
            out_ref[grid_row, pl.ds(slot, 1), :] = jnp.where(slot < live, swept, 0.0)


def pick(core, sub_field, reluctivity, stride, counts, source_cell, target_row):
    cells, rotor = sub_field.shape
    _, grid_rows, slots = source_cell.shape
    pad = 512
    return pl.pallas_call(
        pick_kernel,
        out_shape=[
            jax.ShapeDtypeStruct((grid_rows, slots, rotor), F32),
            jax.ShapeDtypeStruct((1, target_row.size), jnp.int32),
        ],
        in_specs=[SMEM, HBM, HBM, HBM, VMEM, HBM, HBM],
        out_specs=[VMEM, VMEM],
        scratch_shapes=[
            pltpu.SMEM(stride.shape, jnp.int32),
            pltpu.SMEM(counts.shape, jnp.int32),
            pltpu.SMEM(source_cell.shape, jnp.int32),
            pltpu.VMEM((pad + cells, rotor), F32),
            pltpu.VMEM((2, cells, rotor), F32),
            pltpu.SemaphoreType.DMA((15,)),
        ],
        compiler_params=kernel_params(PICK_LIMIT),
        name="pick",
    )(core, stride, counts, source_cell, target_row, sub_field, reluctivity)


def left_lanes(shape):
    return lax.broadcasted_iota(jnp.int32, shape, 1) < shape[1] // 2


def swap_lanes(value):
    return pltpu.roll(value, value.shape[1] // 2, 1)


def packed(own, other):
    half = own.shape[0] // 2
    return jnp.where(
        left_lanes((half, own.shape[1])),
        own[:half] + swap_lanes(other[:half]),
        swap_lanes(own[half:]) + other[half:],
    )


def three_parts(value):
    high, low = split(value)
    rest = (value - high.astype(F32) - low.astype(F32)).astype(BF16)
    return jnp.concatenate([high, low], axis=1), rest


def both_sides(pair):
    return pair.reshape(pair.shape[0] * pair.shape[1], pair.shape[2])


def fill_interface(block, targets_ref, slots, totals):
    pair, rest = three_parts(slots)
    _, rows, width = totals.shape
    row = block * rows + lax.broadcasted_iota(jnp.int32, (rows, slots.shape[0]), 0)
    chosen = jnp.concatenate(
        [jnp.where(row == targets_ref[side], 1.0, 0.0) for side in range(2)], axis=0
    ).astype(BF16)
    both = dot(chosen, pair)
    total = both[:, :width] + both[:, width:] + dot(chosen, rest)
    totals[...] = total.reshape(totals.shape)


def first_kernel(
    core_ref, own_ref, other_ref, received_ref, swapped_ref, out_ref, slots_ref, targets_ref, totals
):
    targets_ref[0] = own_ref[...]
    targets_ref[1] = other_ref[...]
    received, swapped = received_ref[...], swapped_ref[...]
    left = left_lanes(received.shape)
    low = jnp.where(left, received, swap_lanes(swapped))
    high = jnp.where(left, swap_lanes(received), swapped)
    slots = jnp.where(core_ref[0] == 0, low, high)
    slots_ref[...] = slots
    fill_interface(0, targets_ref, slots, totals)
    out_ref[...] = packed(totals[0], totals[1])


def first_residual(core, own_targets, other_targets, received, swapped, rows):
    rotor = received.shape[1]
    return pl.pallas_call(
        first_kernel,
        out_shape=[
            jax.ShapeDtypeStruct((rows // 2, rotor), F32),
            jax.ShapeDtypeStruct(received.shape, F32),
            jax.ShapeDtypeStruct((2, *own_targets.shape), jnp.int32),
        ],
        in_specs=[SMEM] + [VMEM] * 4,
        out_specs=[VMEM] * 3,
        scratch_shapes=[pltpu.VMEM((2, rows, rotor), F32)],
        compiler_params=kernel_params(),
        name="first",
    )(core, own_targets, other_targets, received, swapped)


def split_sides(load, tiles, first, high_ref, low_ref):
    @pl.loop(0, 2)
    def _(side):
        load(first + side).wait()
        high_ref[side], low_ref[side] = split(tiles[first + side])


def fold_kernel(block, with_diag, skip, ahead, *refs):
    earlier = block - 1
    later, count = ahead
    refs = list(refs)
    targets_ref, slots_ref = refs[:2]
    lowers = refs[2:4]
    diags = refs[4:6] if with_diag else []
    at = 4 + len(diags)
    shares = refs[at : at + earlier]
    at += earlier
    carried = refs[at : at + 1] if skip else []
    at += len(carried)
    started_ref, lower_high, lower_low = refs[at : at + 3]
    at += 3
    diag_outs = refs[at : at + 2] if with_diag else []
    at += len(diag_outs)
    ahead_outs = refs[at : at + 1] if count else []
    at += len(ahead_outs)
    totals, tiles, held, sems, share_sems = refs[at : at + 5]
    base = block * (block - 1) // 2

    wanted = [base + j for j in range(skip, block)]
    wanted += [later * (later - 1) // 2 + j for j in range(count)]
    for index, pair in enumerate(wanted):
        for side in range(2):
            at_tile = 2 * index + side
            pltpu.make_async_copy(
                lowers[side].at[pair], tiles.at[at_tile], sems.at[at_tile]
            ).start()
    for j in range(earlier):
        pltpu.make_async_copy(shares[j], held.at[j], share_sems.at[j]).start()

    def loaded(at_tile):
        return pltpu.make_async_copy(lowers[0].at[0], tiles.at[at_tile], sems.at[at_tile])

    if with_diag:
        diag_tiles, diag_sems = refs[-2:]

        def diag_loaded(side):
            return pltpu.make_async_copy(diags[0].at[0], diag_tiles.at[side], diag_sems.at[side])

        for side in range(2):
            pltpu.make_async_copy(
                diags[side].at[earlier], diag_tiles.at[side], diag_sems.at[side]
            ).start()

    fill_interface(block, targets_ref, slots_ref[...], totals)
    for j in range(earlier):
        pltpu.make_async_copy(shares[j], held.at[j], share_sems.at[j]).wait()
    if skip:
        totals[...] = totals[...] + carried[0][...]

    def subtract(total_ref, at_tile, share):
        loaded(at_tile).wait()
        loaded(at_tile + 1).wait()
        high, low = split(both_sides(tiles[pl.ds(at_tile, 2)]))
        total_ref[...] = total_ref[...] - split_product(high, low, held[share]).reshape(
            total_ref.shape
        )

    if earlier > skip:

        @pl.loop(skip, earlier)
        def _(j):
            subtract(totals, 2 * (j - skip), j)

    started_ref[...] = packed(totals[0], totals[1])
    split_sides(loaded, tiles, 2 * (earlier - skip), lower_high, lower_low)
    if count:
        ahead_outs[0][...] = jnp.zeros(totals.shape, F32)

        @pl.loop(0, count)
        def _(j):
            subtract(ahead_outs[0], 2 * (block - skip + j), j)

    if with_diag:
        split_sides(diag_loaded, diag_tiles, 0, *diag_outs)


def fold(block, targets, slots, lowers, diags, shares, carried=(), skip=0, ahead=(0, 0)):
    n_pairs = block - skip + ahead[1]
    _, rows, columns = lowers[0].shape
    rotor = slots.shape[1]
    shapes = [jax.ShapeDtypeStruct((rows // 2, rotor), F32)]
    shapes += [jax.ShapeDtypeStruct((2, rows, columns), BF16)] * 2
    scratch = [
        pltpu.VMEM((2, rows, rotor), F32),
        pltpu.VMEM((2 * n_pairs, rows, columns), F32),
        pltpu.VMEM((max(block - 1, 1), columns, rotor), F32),
        pltpu.SemaphoreType.DMA((2 * n_pairs,)),
        pltpu.SemaphoreType.DMA((block,)),
    ]
    if diags:
        _, out_rows, depth = diags[0].shape
        shapes += [jax.ShapeDtypeStruct((2, out_rows, depth), BF16)] * 2
        scratch += [pltpu.VMEM((2, out_rows, depth), F32), pltpu.SemaphoreType.DMA((2,))]
    if ahead[1]:
        shapes += [jax.ShapeDtypeStruct((2, rows, rotor), F32)]
    return pl.pallas_call(
        functools.partial(fold_kernel, block, bool(diags), skip, ahead),
        out_shape=shapes,
        in_specs=[VMEM] * 2 + [HBM] * (2 + len(diags)) + [VMEM] * (len(shares) + len(carried)),
        out_specs=[VMEM] * len(shapes),
        scratch_shapes=scratch,
        compiler_params=kernel_params(WIDE_LIMIT),
        cost_estimate=pl.CostEstimate(
            flops=12 * n_pairs * rows * columns * rotor,
            bytes_accessed=8 * (n_pairs + 1) * rows * columns,
            transcendentals=0,
        ),
        name="fold",
    )(targets, slots, *lowers, *diags, *shares, *carried)


def prepare_kernel(block, own_hbm, other_hbm, high_ref, low_ref, diags, sems):
    for side, hbm in enumerate((own_hbm, other_hbm)):
        pltpu.make_async_copy(hbm.at[block], diags.at[side], sems.at[side]).start()

    def loaded(side):
        return pltpu.make_async_copy(own_hbm.at[block], diags.at[side], sems.at[side])

    split_sides(loaded, diags, 0, high_ref, low_ref)


def prepare(block, diags):
    _, out_rows, depth = diags[0].shape
    return pl.pallas_call(
        functools.partial(prepare_kernel, block),
        out_shape=[jax.ShapeDtypeStruct((2, out_rows, depth), BF16)] * 2,
        in_specs=[HBM] * 2,
        out_specs=[VMEM] * 2,
        scratch_shapes=[
            pltpu.VMEM((2, out_rows, depth), F32),
            pltpu.SemaphoreType.DMA((2,)),
        ],
        compiler_params=kernel_params(WIDE_LIMIT),
        cost_estimate=pl.CostEstimate(
            flops=8 * out_rows * depth,
            bytes_accessed=16 * out_rows * depth,
            transcendentals=0,
        ),
        name="prepare",
    )(*diags)


def lower_kernel(share_ref, high_ref, low_ref, started_ref, out_ref):
    value = split_product(both_sides(high_ref[...]), both_sides(low_ref[...]), share_ref[...])
    rows = high_ref.shape[1]
    out_ref[...] = started_ref[...] - packed(value[:rows], value[rows:])


def lower_product(share, tiles, started):
    return pl.pallas_call(
        lower_kernel,
        out_shape=jax.ShapeDtypeStruct(started.shape, F32),
        in_specs=[VMEM] * 4,
        out_specs=VMEM,
        compiler_params=kernel_params(),
        name="lower",
    )(share, *tiles, started)


def diag_kernel(*refs):
    *residual_refs, high_ref, low_ref, out_ref = refs
    residual = residual_refs[0][...]
    for ref in residual_refs[1:]:
        residual = residual + ref[...]
    turned = swap_lanes(residual)
    left = left_lanes(residual.shape)
    on_left = jnp.concatenate(
        [jnp.where(left, residual, 0.0), jnp.where(left, turned, 0.0)], axis=0
    )
    on_right = jnp.concatenate(
        [jnp.where(left, 0.0, turned), jnp.where(left, 0.0, residual)], axis=0
    )
    out_ref[...] = split_product(high_ref[0], low_ref[0], on_left) + split_product(
        high_ref[1], low_ref[1], on_right
    )


def diag_product(residuals, tiles):
    return pl.pallas_call(
        diag_kernel,
        out_shape=jax.ShapeDtypeStruct((tiles[0].shape[1], residuals[0].shape[1]), F32),
        in_specs=[VMEM] * (len(residuals) + 2),
        out_specs=VMEM,
        compiler_params=kernel_params(),
        name="diag",
    )(*residuals, *tiles)


def piece_kernel(parts_ref, piece_ref, copies_ref):
    piece = jnp.sum(parts_ref[...], axis=0)
    piece_ref[...] = piece
    for peer in range(copies_ref.shape[0]):
        copies_ref[peer] = piece


def piece_and_copies(parts):
    return pl.pallas_call(
        piece_kernel,
        out_shape=[
            jax.ShapeDtypeStruct(parts.shape[1:], F32),
            jax.ShapeDtypeStruct(parts.shape, F32),
        ],
        in_specs=[VMEM],
        out_specs=[VMEM, VMEM],
        compiler_params=kernel_params(),
        name="piece",
    )(parts)


def join_kernel(*refs):
    *piece_refs, out_ref = refs
    for block, piece_ref in enumerate(piece_refs):
        out_ref[block] = piece_ref[...]


def joined(pieces):
    return pl.pallas_call(
        join_kernel,
        out_shape=jax.ShapeDtypeStruct((len(pieces), *pieces[0].shape), F32),
        in_specs=[VMEM] * len(pieces),
        out_specs=VMEM,
        compiler_params=kernel_params(),
        name="join",
    )(*pieces)


def stacked_kernel(core_ref, early_ref, early_other_ref, last_ref, last_other_ref, out_ref):
    left = left_lanes(last_ref.shape)
    first_core = core_ref[0] == 0
    early = early_ref.shape[0]
    for block in range(early + 1):
        own = early_ref[block] if block < early else last_ref[...]
        other = early_other_ref[block] if block < early else last_other_ref[...]
        rows = jnp.where(left, own, other)
        out_ref[block] = jnp.where(first_core, rows, swap_lanes(rows))


def stacked(core, early, early_other, last, last_other):
    return pl.pallas_call(
        stacked_kernel,
        out_shape=jax.ShapeDtypeStruct((early.shape[0] + 1, *last.shape), F32),
        in_specs=[SMEM] + [VMEM] * 4,
        out_specs=VMEM,
        compiler_params=kernel_params(),
        name="stacked",
    )(core, early, early_other, last, last_other)


def other_core(value):
    peers = lax.axis_size("col")
    return lax.ppermute(value, "col", [(i, i ^ 1) for i in range(peers)])


def along_x(value):
    peers = lax.axis_size("col")
    return [value] + [
        lax.ppermute(value, "col", [(i, i ^ apart) for i in range(peers)])
        for apart in (2, 6, 4)
    ]


def per_row(value):
    return lax.all_to_all(value, "row", 0, 0, tiled=True)


def per_device(
    sub_field, reluctivity, stride, counts, source_cell, target_row, lower_tiles, diag_inverse
):
    blocks = diag_inverse.shape[0]
    tile_rows = lower_tiles.shape[1]
    rotor = sub_field.shape[1]
    peers = lax.axis_size("row")
    core = (lax.axis_index("col") % 2).astype(jnp.int32).reshape(1)
    other_diag = other_core(diag_inverse)
    picked, targets = pick(
        core, sub_field, reluctivity, stride, counts, source_cell, target_row[0, 0]
    )
    other_targets = other_core(targets)
    received = per_row(picked).reshape(-1, rotor)
    received, other_diag = lax.optimization_barrier((received, other_diag))
    diags = (diag_inverse, other_diag)

    shares = []
    pieces = []
    waiting = {}
    residual, slots, targets = first_residual(
        core, targets, other_targets, received, other_core(received), tile_rows
    )
    own_lower, slots = lax.optimization_barrier((lower_tiles, slots))
    lowers = (lower_tiles, other_core(own_lower))
    for block in range(blocks):
        later = block + 1
        if later == blocks:
            residual, pieces = lax.optimization_barrier((residual, pieces))
        residuals = along_x(residual)
        if later < blocks:
            ahead = {2: (blocks - 2, 1), 3: (blocks - 1, 2)}.get(later, (0, 0))
            carried = waiting.pop(later, None)
            started, lower_high, lower_low, *diag_tiles = fold(
                later,
                targets,
                slots,
                lowers,
                diags if block else (),
                shares,
                () if carried is None else (carried[0],),
                0 if carried is None else carried[1],
                ahead,
            )
            if ahead[1]:
                waiting[ahead[0]] = (diag_tiles.pop(), ahead[1])
        if block == 0 or later == blocks:
            diag_tiles = prepare(block, diags)
        if later == blocks:
            early = joined(pieces)
            diag_tiles, early, early_other = lax.optimization_barrier(
                (diag_tiles, early, other_core(early))
            )
        parts = per_row(diag_product(residuals, diag_tiles).reshape(peers, -1, rotor))
        if later < blocks:
            piece, copies = piece_and_copies(parts)
            pieces.append(piece)
            share = per_row(copies).reshape(-1, rotor)
            shares.append(share)
            residual = lower_product(share, (lower_high, lower_low), started)
    last = jnp.sum(parts, axis=0)
    return stacked(core, early, early_other, last, other_core(last))[:, None]


def solution(mesh):
    placed = (
        P(("row", "col"), None),
        P(None, ("row", "col"), None),
        P(("row", "col")),
        P(("row", "col"), None),
        P(("row", "col"), None, None),
        P("row", "col", None, None),
        P(None, "row", "col"),
        P(None, "col", "row"),
    )
    return jax.shard_map(
        per_device,
        mesh=mesh,
        in_specs=placed,
        out_specs=P(None, "col", "row", None),
        check_vma=False,
    )
```
